256 devices in a mesh: member: 2 (over y_lo), lat: 16 (over y_hi, z), lon: 8 (over x, core).
Axes of the slice: x: 4, y: 4 (y_hi: 2, y_lo: 2; y = y_hi * 2 + y_lo), z: 8, core: 2. Of those that a mesh axis runs over, the one named last changes fastest.
Arguments:
- features: bfloat16 [1024, 128, 512], P(('member', 'lat'), 'lon'), parts along dimension 0, may hold values from -12 to 12
- grad_out: bfloat16 [1024, 128, 512], P(('member', 'lat'), 'lon'), parts along dimension 0, may hold values from -6 to 6
- w_query: bfloat16 [512, 512], replicated, may hold values from -0.25 to 0.25
- w_key: bfloat16 [512, 512], replicated, may hold values from -0.25 to 0.25
- w_value: bfloat16 [512, 512], replicated, may hold values from -0.25 to 0.25
- w_out: bfloat16 [512, 512], replicated, may hold values from -0.25 to 0.25
- block_lists: int32 [8, 8, 4], replicated, may hold values from 0 to 7, all different within a row
Outputs:
- output: bfloat16 [1024, 128, 512], P(('member', 'lat'), 'lon'), parts along dimension 0
- grad_in: bfloat16 [1024, 128, 512], P(('member', 'lat'), 'lon'), parts along dimension 0
- grad_wq: float32 [1024, 512], P('member'), parts along dimension 0
- grad_wk: float32 [1024, 512], P('member'), parts along dimension 0
- grad_wv: float32 [1024, 512], P('member'), parts along dimension 0
- grad_wo: float32 [1024, 512], P('member'), parts along dimension 0
The draws below stay inside these ranges and needn't reach their ends.
There are 2 independent parts, one for each index of `member`. The reference program is written for one: setup_inputs(seed, part) draws one part's arguments, and reference() takes and returns one part's arrays. A program takes and returns all parts, laid end to end along the dimension named above; an argument that names none is the same for every part. Nothing has to cross between parts.
Inputs may be any that keep to these rules, and one draw needn't show every extreme that they name: `block_lists`: each row names 4 different key blocks, and every block is named somewhere.
All inputs are finite; a program needn't handle non-finite values.
Results may differ from the reference program's by a relative error of at most 0.0094.
Values may be sent and summed in bfloat16 or wider, within the bound.
No kernel may reach another device: no remote copies, remote signals or barrier semaphores. Data moves between devices by JAX's collectives and lax.ppermute only.
A program may use at most 128 MiB of HBM per device.

```python
import math
import jax
import jax.numpy as jnp
from jax import lax

D = 512
HEADS = 8
BLK = 64
HEAD_DIM = 64
NLAT = 512
NLON = 128
NB = 8
KB = 4
CELLS = 65536


def draw_features(key, part):
    key = jax.random.fold_in(key, 11)
    base = jax.random.normal(key, (NLAT, NLON, D), jnp.float32)
    return jnp.clip(base, -4.0, 4.0).astype(jnp.bfloat16)


def block_levels(key, dims, shards, low, largest):
    gain = 1.0
    for axis_at, parts in shards:
        draws = jax.random.uniform(jax.random.fold_in(jax.random.fold_in(key, 6), axis_at), (parts,), jnp.float32, low / len(shards), largest / len(shards))
        gain = gain * jnp.repeat(jnp.exp(draws), dims[axis_at] // parts).reshape((-1,) + (1,) * (len(dims) - 1 - axis_at))
    return gain


def distinct(stream_key, rows, count, top, lift):
    order = jax.random.permutation(jax.random.fold_in(stream_key, 1), count)
    pull = order
    for power in range(3):
        pull = pull * pull // count
    pull = pull * lift // count
    lots = jax.random.randint(jax.random.fold_in(stream_key, 2), (rows, count), 0, 4096) + pull
    fixed_rows = jax.random.permutation(jax.random.fold_in(stream_key, 3), rows)[jnp.arange(count) % rows]
    lots = jnp.where(jnp.arange(rows)[:, None] == fixed_rows[None, :], 1 << 14, lots)
    score = lots * count + jnp.arange(count)
    return lax.top_k(score.astype(jnp.int32), top)[1].astype(jnp.int32)


def scatter_about(stream_key, extent, scale, reach, cuts=(), held_as=jnp.bfloat16):
    loudness = block_levels(stream_key, extent, cuts, -0.22, 0.18) if cuts else 1.0
    drawn = jax.random.normal(stream_key, extent, jnp.float32) * scale * loudness
    return jnp.minimum(jnp.maximum(drawn, -reach), reach).astype(held_as)


def setup_inputs(seed: int = 0, part: int = 0) -> dict:
    streams_of = jax.random.split(jax.random.key(seed), 8)
    part_splits = jax.random.split(jax.random.fold_in(streams_of[7], part), 8)
    return {
        "features": draw_features(jax.random.fold_in(jax.random.fold_in(streams_of[7], part), 71), part),
        "grad_out": scatter_about(part_splits[1], (NLAT, NLON, D), 1.0, 6.0, ((0, 16), (1, 8))),
        "w_query": scatter_about(streams_of[2], (D, D), D ** -0.5, 0.25),
        "w_key": scatter_about(streams_of[3], (D, D), D ** -0.5, 0.25),
        "w_value": scatter_about(streams_of[4], (D, D), D ** -0.5, 0.25),
        "w_out": scatter_about(streams_of[5], (D, D), D ** -0.5, 0.25),
        "block_lists": distinct(streams_of[6], HEADS * NB, NB, KB, 0).reshape((HEADS, NB, KB)),
    }


def block_mask(block_lists):
    names = jnp.arange(NB, dtype=jnp.int32)
    allowed = jnp.any(block_lists[:, :, :, None] == names[None, None, None, :], axis=2)
    allowed = jnp.broadcast_to(allowed[:, :, None, :, None], (HEADS, NB, BLK, NB, BLK))
    return allowed.reshape(HEADS, NLAT, NLAT)

def column_pass(tensors, allowed, factor):
    query, keys, values, grad_attn = tensors
    shape = (NLAT, HEADS, HEAD_DIM)
    q_heads = query.reshape(shape).astype(jnp.float32)
    k_heads = keys.reshape(shape).astype(jnp.float32)
    v_heads = values.reshape(shape).astype(jnp.float32)
    g_heads = grad_attn.reshape(shape).astype(jnp.float32)
    scores = jnp.einsum('ihd,jhd->hij', q_heads, k_heads) * factor
    scores = jnp.where(allowed, scores, jnp.float32(-1e+30))
    top = lax.optimization_barrier(jnp.max(scores, axis=2, keepdims=True))
    expo = jnp.exp(scores - top)
    probs = expo / lax.optimization_barrier(jnp.sum(expo, axis=2, keepdims=True))
    probs_low = probs.astype(jnp.bfloat16).astype(jnp.float32)
    attended = jnp.einsum('hij,jhd->ihd', probs_low, v_heads).astype(jnp.bfloat16).reshape(NLAT, D)
    dprobs = jnp.einsum('ihd,jhd->hij', g_heads, v_heads)
    dvalues = jnp.einsum('hij,ihd->jhd', probs_low, g_heads).astype(jnp.bfloat16).reshape(NLAT, D)
    delta = lax.optimization_barrier(jnp.sum(probs * dprobs, axis=2, keepdims=True))
    dscores = (probs * (dprobs - delta) * factor).astype(jnp.bfloat16).astype(jnp.float32)
    dquery = jnp.einsum('hij,jhd->ihd', dscores, k_heads).astype(jnp.bfloat16).reshape(NLAT, D)
    dkeys = jnp.einsum('hij,ihd->jhd', dscores, q_heads).astype(jnp.bfloat16).reshape(NLAT, D)
    return (attended, dquery, dkeys, dvalues)

def reference(features, grad_out, w_query, w_key, w_value, w_out, block_lists):
    flat = features.reshape(NLAT * NLON, D)
    grad_flat = grad_out.reshape(NLAT * NLON, D)
    query = jnp.dot(flat, w_query, preferred_element_type=jnp.float32).astype(jnp.bfloat16)
    keys = jnp.dot(flat, w_key, preferred_element_type=jnp.float32).astype(jnp.bfloat16)
    values = jnp.dot(flat, w_value, preferred_element_type=jnp.float32).astype(jnp.bfloat16)
    grad_attn = jnp.dot(grad_flat, w_out.T, preferred_element_type=jnp.float32).astype(jnp.bfloat16)
    allowed = block_mask(block_lists)
    factor = 1.0 / math.sqrt(HEAD_DIM)

    def to_columns(array):
        return jnp.swapaxes(array.reshape(NLAT, NLON, D), 0, 1)

    def from_columns(array):
        return jnp.swapaxes(array, 0, 1).reshape(NLAT * NLON, D)
    results = lax.map(lambda tensors: column_pass(tensors, allowed, factor), (to_columns(query), to_columns(keys), to_columns(values), to_columns(grad_attn)))
    attended, dquery, dkeys, dvalues = [from_columns(item) for item in results]
    output = flat.astype(jnp.float32) + jnp.dot(attended, w_out, preferred_element_type=jnp.float32)
    output = output.astype(jnp.bfloat16).reshape(NLAT, NLON, D)
    grad_in = grad_flat.astype(jnp.float32)
    grad_in = grad_in + jnp.dot(dquery, w_query.T, preferred_element_type=jnp.float32)
    grad_in = grad_in + jnp.dot(dkeys, w_key.T, preferred_element_type=jnp.float32)
    grad_in = grad_in + jnp.dot(dvalues, w_value.T, preferred_element_type=jnp.float32)
    grad_in = grad_in.astype(jnp.bfloat16).reshape(NLAT, NLON, D)
    norm = 1.0 / math.sqrt(CELLS)
    grad_wq = jnp.dot(flat.T, dquery, preferred_element_type=jnp.float32) * norm
    grad_wk = jnp.dot(flat.T, dkeys, preferred_element_type=jnp.float32) * norm
    grad_wv = jnp.dot(flat.T, dvalues, preferred_element_type=jnp.float32) * norm
    grad_wo = jnp.dot(attended.T, grad_flat, preferred_element_type=jnp.float32) * norm
    return (output, grad_in, grad_wq, grad_wk, grad_wv, grad_wo)
```

```python
import functools
import math

import jax
import jax.numpy as jnp
from jax import lax
from jax.experimental import pallas as pl
from jax.experimental.pallas import tpu as pltpu
from jax.sharding import PartitionSpec as P

HEADS = 8
BLK = 64
CORES = 2
BF16 = jnp.bfloat16
F32 = jnp.float32
NT = (((1,), (1,)), ((), ()))


def dot(left, right):
    return jnp.dot(left, right, preferred_element_type=F32)


def dot_nt(left, right):
    return lax.dot_general(left, right, NT, preferred_element_type=F32)


def column_kernel(
    norm,
    spots,
    place_ref,
    xg_ref,
    w_ref,
    wt_ref,
    wo_ref,
    wot_ref,
    bias_ref,
    og_ref,
    mine_ref,
    send_ref,
    rows_ref,
    cols_ref,
    ga_ref,
    gat_ref,
    left_ref,
    right_ref,
    dqt_ref,
):
    rows, width = ga_ref.shape
    head_dim = width // HEADS
    pair = 2 * head_dim
    factor = 1.0 / math.sqrt(head_dim)
    scale = factor * math.log2(math.e)
    x = xg_ref[:, 0].reshape(rows, width)
    g = xg_ref[:, 1].reshape(rows, width)
    left_ref[0] = x.T
    right_ref[3] = g

    for part in range(3):
        span = slice(part * width, (part + 1) * width)
        rows_ref[:, span] = dot(x, w_ref[:, span]).astype(BF16)
        cols_ref[span, :] = dot_nt(wt_ref[span, :], x).astype(BF16)
    ga_ref[...] = dot(g, wot_ref[...]).astype(BF16)
    gat_ref[...] = dot_nt(wo_ref[...], g).astype(BF16)

    first = lax.broadcasted_iota(jnp.int32, (rows, pair), 1) < head_dim
    blank = jnp.zeros((head_dim, rows), BF16)

    def pair_step(p, carry):
        at = pl.multiple_of(p * pair, pair)
        q_pair = rows_ref[:, pl.ds(at, pair)]
        k_pair = rows_ref[:, pl.ds(pl.multiple_of(width + at, pair), pair)]
        v_pair = rows_ref[:, pl.ds(pl.multiple_of(2 * width + at, pair), pair)]
        g_pair = ga_ref[:, pl.ds(at, pair)]
        dvs, dks = [], []
        for odd in range(2):
            here = pl.multiple_of(at + odd * head_dim, head_dim)
            qt = cols_ref[pl.ds(here, head_dim), :]
            kt = cols_ref[pl.ds(pl.multiple_of(width + here, head_dim), head_dim), :]
            vt = cols_ref[pl.ds(pl.multiple_of(2 * width + here, head_dim), head_dim), :]
            gt = gat_ref[pl.ds(here, head_dim), :]
            q_wide = jnp.concatenate([blank, qt] if odd else [qt, blank], axis=0)
            g_wide = jnp.concatenate([blank, gt] if odd else [gt, blank], axis=0)
            bias = bias_ref[2 * p + odd]
            scores = dot(k_pair, q_wide).reshape(rows // BLK, BLK, rows) + bias[:, None, :]
            scores = scores.reshape(rows, rows)
            top = jnp.max(scores, axis=0, keepdims=True)
            expo = jnp.exp2((scores - top) * scale)
            probs = expo * (1.0 / jnp.sum(expo, axis=0, keepdims=True))
            low = probs.astype(BF16)
            left_ref[1, pl.ds(here, head_dim), :] = dot(vt, low).astype(BF16)
            dvs.append(dot(low, g_pair))
            dprobs = dot(v_pair, g_wide)
            delta = jnp.sum(probs * dprobs, axis=0, keepdims=True)
            dscores = (probs * (dprobs - delta) * factor).astype(BF16)
            dqt_ref[pl.ds(here, head_dim), :] = dot(kt, dscores).astype(BF16)
            dks.append(dot(dscores, q_pair))
        right_ref[1, :, pl.ds(at, pair)] = jnp.where(first, dks[0], dks[1]).astype(BF16)
        right_ref[2, :, pl.ds(at, pair)] = jnp.where(first, dvs[0], dvs[1]).astype(BF16)
        return carry

    lax.fori_loop(0, HEADS // 2, pair_step, 0)
    right_ref[0] = dqt_ref[...].T
    attended = left_ref[1].T
    output = x.astype(F32) + dot(attended, wo_ref[...])
    og_ref[:, 0] = output.astype(BF16).reshape(og_ref.shape[0], og_ref.shape[2], width)
    grad_in = g.astype(F32) + dot(right_ref[0], wt_ref[:width, :])
    grad_in = grad_in + dot(right_ref[1], wt_ref[width : 2 * width, :])
    grad_in = grad_in + dot(right_ref[2], wt_ref[2 * width :, :])
    og_ref[:, 1] = grad_in.astype(BF16).reshape(og_ref.shape[0], og_ref.shape[2], width)

    core, spot = place_ref[0], place_ref[1]
    high = mine_ref.shape[1]
    per = width // high

    def grad_step(slot, carry):
        chunk = lax.rem(spot + slot, spots)
        for half, out_ref in enumerate((mine_ref, send_ref)):
            which = lax.rem(core + half, 2) * (spots // per) + chunk // per
            start = pl.multiple_of(lax.rem(chunk, per) * high, high)
            lhs = left_ref[which // 3, pl.ds(start, high), :]
            out_ref[slot] = dot(lhs, right_ref[which]) * norm
        return carry

    lax.fori_loop(0, spots, grad_step, 0)


def column_pass(xg, w, wt, wo, wot, bias, place, norm, spots):
    lat, _, lat_rows, width = xg.shape
    rows = lat * lat_rows
    high = 4 * width // CORES // spots
    whole = pl.BlockSpec(memory_space=pltpu.VMEM)
    return pl.pallas_call(
        functools.partial(column_kernel, norm, spots),
        out_shape=(
            jax.ShapeDtypeStruct(xg.shape, BF16),
            jax.ShapeDtypeStruct((spots, high, width), F32),
            jax.ShapeDtypeStruct((spots, high, width), F32),
        ),
        in_specs=[pl.BlockSpec(memory_space=pltpu.SMEM)] + [whole] * 6,
        out_specs=(whole,) * 3,
        scratch_shapes=[
            pltpu.VMEM((rows, 3 * width), BF16),
            pltpu.VMEM((3 * width, rows), BF16),
            pltpu.VMEM((rows, width), BF16),
            pltpu.VMEM((width, rows), BF16),
            pltpu.VMEM((2, width, rows), BF16),
            pltpu.VMEM((4, rows, width), BF16),
            pltpu.VMEM((width, rows), BF16),
        ],
        compiler_params=pltpu.CompilerParams(vmem_limit_bytes=48 * 1024 * 1024),
    )(place, xg, w, wt, wo, wot, bias)


def spread_kernel(spots, place_ref, *refs):
    ins, outs = refs[: 2 * spots], refs[2 * spots :]
    core, spot = place_ref[0], place_ref[1]
    high = ins[0].shape[0]
    per = outs[0].shape[0] // high
    for chunk in range(CORES * spots):
        half, rest = chunk // spots, chunk % spots
        out_ref = outs[chunk // per]
        start = (chunk % per) * high
        slot = lax.rem(rest - spot + spots, spots)
        side = jnp.where(core == half, 0, 1)
        for at, in_ref in enumerate(ins):

            @pl.when(side * spots + slot == at)
            def _():
                out_ref[start : start + high, :] = in_ref[...].astype(F32)


def spread(parts, place, width):
    whole = pl.BlockSpec(memory_space=pltpu.VMEM)
    return pl.pallas_call(
        functools.partial(spread_kernel, len(parts) // 2),
        out_shape=(jax.ShapeDtypeStruct((width, width), F32),) * 4,
        in_specs=[pl.BlockSpec(memory_space=pltpu.SMEM)] + [whole] * len(parts),
        out_specs=(whole,) * 4,
        compiler_params=pltpu.CompilerParams(vmem_limit_bytes=32 * 1024 * 1024),
    )(place, *parts)


def mask_bias(block_lists, rows):
    heads, blocks, listed = block_lists.shape
    names = jnp.arange(blocks, dtype=jnp.int32)
    allowed = jnp.any(block_lists[:, :, :, None] == names[None, None, None, :], axis=2)
    bias = jnp.where(jnp.swapaxes(allowed, 1, 2), 0.0, -1e30).astype(F32)
    return jnp.repeat(bias, rows // blocks, axis=2)


def swap_core(item, lon):
    return lax.ppermute(item, "lon", [(i, i ^ 1) for i in range(lon)])


def shift_chip(item, lon, by):
    return lax.ppermute(item, "lon", [(i, (i + by * CORES) % lon) for i in range(lon)])


def per_device(features, grad_out, w_query, w_key, w_value, w_out, block_lists):
    lat_rows, lon_cols, width = features.shape
    lat, lon = lax.axis_size("lat"), lax.axis_size("lon")
    spots = lon // CORES
    norm = 1.0 / math.sqrt(lat_rows * lon_cols * lat * lon)
    index = lax.axis_index("lon")
    place = jnp.stack([lax.rem(index, CORES), index // CORES]).astype(jnp.int32)
    w = jnp.concatenate([w_query, w_key, w_value], axis=1)
    bias = mask_bias(block_lists, lat * lat_rows)

    tiles = jnp.stack([features, grad_out]).transpose(2, 0, 1, 3)
    xg = lax.all_to_all(tiles, "lat", 0, 0, tiled=True)
    og, mine, send = column_pass(xg, w, w.T, w_out, w_out.T, bias, place, norm, spots)
    back = lax.all_to_all(og, "lat", 0, 0, tiled=True)
    back = back.transpose(1, 2, 0, 3)

    taken = swap_core(send, lon)
    total = mine[0] + taken[0]
    others = [shift_chip(mine[k] + taken[k], lon, k) for k in range(1, spots)]
    for item in others:
        total = total + item
    total = total.reshape(lat, -1, width)
    total = jnp.sum(lax.all_to_all(total, "lat", 0, 0, tiled=True), axis=0)
    total = jnp.broadcast_to(total.astype(BF16)[None], (lat,) + total.shape)
    own = lax.all_to_all(total, "lat", 0, 0, tiled=True).reshape(-1, width)
    near = [own] + [shift_chip(own, lon, spots - k) for k in range(1, spots)]
    far = [swap_core(item, lon) for item in near]
    grads = spread(near + far, place, width)
    return (back[0], back[1]) + tuple(grads)


def solution(mesh):
    tile = P(("member", "lat"), "lon", None)
    in_specs = (tile, tile, P(), P(), P(), P(), P())
    out_specs = (tile, tile) + (P("member", None),) * 4
    return jax.shard_map(
        per_device, mesh=mesh, in_specs=in_specs, out_specs=out_specs, check_vma=False
    )
```

```python
import functools
import math

import jax
import jax.numpy as jnp
from jax import lax
from jax.experimental import pallas as pl
from jax.experimental.pallas import tpu as pltpu
from jax.sharding import PartitionSpec as P

HEADS = 8
BLK = 64
CORES = 2
BF16 = jnp.bfloat16
F32 = jnp.float32
NT = (((1,), (1,)), ((), ()))


def dot(left, right):
    return jnp.dot(left, right, preferred_element_type=F32)


def dot_nt(left, right):
    return lax.dot_general(left, right, NT, preferred_element_type=F32)


def column_kernel(
    norm,
    spots,
    place_ref,
    xg_ref,
    w_ref,
    wt_ref,
    wo_ref,
    wot_ref,
    bias_ref,
    og_ref,
    mine_ref,
    send_ref,
    rows_ref,
    cols_ref,
    ga_ref,
    gat_ref,
    left_ref,
    right_ref,
    dqt_ref,
):
    rows, width = ga_ref.shape
    head_dim = width // HEADS
    pair = 2 * head_dim
    factor = 1.0 / math.sqrt(head_dim)
    scale = factor * math.log2(math.e)
    x = xg_ref[:, 0].reshape(rows, width)
    g = xg_ref[:, 1].reshape(rows, width)
    left_ref[0] = x.T
    right_ref[3] = g

    for part in range(3):
        span = slice(part * width, (part + 1) * width)
        rows_ref[:, span] = dot(x, w_ref[:, span]).astype(BF16)
        cols_ref[span, :] = dot_nt(wt_ref[span, :], x).astype(BF16)
    ga_ref[...] = dot(g, wot_ref[...]).astype(BF16)
    gat_ref[...] = dot_nt(wo_ref[...], g).astype(BF16)

    first = lax.broadcasted_iota(jnp.int32, (rows, pair), 1) < head_dim
    blank = jnp.zeros((head_dim, rows), BF16)

    def pair_step(p, carry):
        at = pl.multiple_of(p * pair, pair)
        q_pair = rows_ref[:, pl.ds(at, pair)]
        k_pair = rows_ref[:, pl.ds(pl.multiple_of(width + at, pair), pair)]
        v_pair = rows_ref[:, pl.ds(pl.multiple_of(2 * width + at, pair), pair)]
        g_pair = ga_ref[:, pl.ds(at, pair)]
        dvs, dks = [], []
        for odd in range(2):
            here = pl.multiple_of(at + odd * head_dim, head_dim)
            qt = cols_ref[pl.ds(here, head_dim), :]
            kt = cols_ref[pl.ds(pl.multiple_of(width + here, head_dim), head_dim), :]
            vt = cols_ref[pl.ds(pl.multiple_of(2 * width + here, head_dim), head_dim), :]
            gt = gat_ref[pl.ds(here, head_dim), :]
            q_wide = jnp.concatenate([blank, qt] if odd else [qt, blank], axis=0)
            g_wide = jnp.concatenate([blank, gt] if odd else [gt, blank], axis=0)
            bias = bias_ref[2 * p + odd]
            scores = dot(k_pair, q_wide).reshape(rows // BLK, BLK, rows) + bias[:, None, :]
            scores = scores.reshape(rows, rows)
            top = jnp.max(scores, axis=0, keepdims=True)
            expo = jnp.exp2((scores - top) * scale)
            probs = expo * (1.0 / jnp.sum(expo, axis=0, keepdims=True))
            low = probs.astype(BF16)
            left_ref[1, pl.ds(here, head_dim), :] = dot(vt, low).astype(BF16)
            dvs.append(dot(low, g_pair))
            dprobs = dot(v_pair, g_wide)
            delta = jnp.sum(probs * dprobs, axis=0, keepdims=True)
            dscores = (probs * (dprobs - delta) * factor).astype(BF16)
            dqt_ref[pl.ds(here, head_dim), :] = dot(kt, dscores).astype(BF16)
            dks.append(dot(dscores, q_pair))
        right_ref[1, :, pl.ds(at, pair)] = jnp.where(first, dks[0], dks[1]).astype(BF16)
        right_ref[2, :, pl.ds(at, pair)] = jnp.where(first, dvs[0], dvs[1]).astype(BF16)
        return carry

    lax.fori_loop(0, HEADS // 2, pair_step, 0)
    right_ref[0] = dqt_ref[...].T
    attended = left_ref[1].T
    output = x.astype(F32) + dot(attended, wo_ref[...])
    og_ref[:, 0] = output.astype(BF16).reshape(og_ref.shape[0], og_ref.shape[2], width)
    grad_in = g.astype(F32) + dot(right_ref[0], wt_ref[:width, :])
    grad_in = grad_in + dot(right_ref[1], wt_ref[width : 2 * width, :])
    grad_in = grad_in + dot(right_ref[2], wt_ref[2 * width :, :])
    og_ref[:, 1] = grad_in.astype(BF16).reshape(og_ref.shape[0], og_ref.shape[2], width)

    core, spot = place_ref[0], place_ref[1]
    high = mine_ref.shape[1]
    per = width // high

    def grad_step(slot, carry):
        chunk = lax.rem(spot + slot, spots)
        for half, out_ref in enumerate((mine_ref, send_ref)):
            which = lax.rem(core + half, 2) * (spots // per) + chunk // per
            start = pl.multiple_of(lax.rem(chunk, per) * high, high)
            lhs = left_ref[which // 3, pl.ds(start, high), :]
            out_ref[slot] = dot(lhs, right_ref[which]) * norm
        return carry

    lax.fori_loop(0, spots, grad_step, 0)


def column_pass(xg, w, wt, wo, wot, bias, place, norm, spots):
    lat, _, lat_rows, width = xg.shape
    rows = lat * lat_rows
    high = 4 * width // CORES // spots
    whole = pl.BlockSpec(memory_space=pltpu.VMEM)
    return pl.pallas_call(
        functools.partial(column_kernel, norm, spots),
        out_shape=(
            jax.ShapeDtypeStruct(xg.shape, BF16),
            jax.ShapeDtypeStruct((spots, high, width), F32),
            jax.ShapeDtypeStruct((spots, high, width), F32),
        ),
        in_specs=[pl.BlockSpec(memory_space=pltpu.SMEM)] + [whole] * 6,
        out_specs=(whole,) * 3,
        scratch_shapes=[
            pltpu.VMEM((rows, 3 * width), BF16),
            pltpu.VMEM((3 * width, rows), BF16),
            pltpu.VMEM((rows, width), BF16),
            pltpu.VMEM((width, rows), BF16),
            pltpu.VMEM((2, width, rows), BF16),
            pltpu.VMEM((4, rows, width), BF16),
            pltpu.VMEM((width, rows), BF16),
        ],
        compiler_params=pltpu.CompilerParams(vmem_limit_bytes=48 * 1024 * 1024),
    )(place, xg, w, wt, wo, wot, bias)


def settle_kernel(back_ref, mine_ref, taken_ref, *refs):
    others, out_ref = refs[:-1], refs[-1]
    total = mine_ref[0] + taken_ref[0]
    for other_ref in others:
        total = total + other_ref[...]
    out_ref[...] = total.reshape(out_ref.shape)


def settle(back, mine, taken, others, lat):
    _, high, width = mine.shape
    slot = pl.BlockSpec((1, high, width), lambda i: (0, 0, 0))
    chunk = pl.BlockSpec((high, width), lambda i: (0, 0))
    shape = (lat, high // lat, width)
    return pl.pallas_call(
        settle_kernel,
        grid=(1,),
        out_shape=jax.ShapeDtypeStruct(shape, F32),
        in_specs=[pl.BlockSpec(memory_space=pl.ANY), slot, slot] + [chunk] * len(others),
        out_specs=pl.BlockSpec(shape, lambda i: (0, 0, 0)),
        compiler_params=pltpu.CompilerParams(vmem_limit_bytes=32 * 1024 * 1024),
    )(back, mine, taken, *others)


def spread_kernel(spots, place_ref, *refs):
    ins, outs = refs[: 2 * spots], refs[2 * spots :]
    core, spot = place_ref[0], place_ref[1]
    high = ins[0].shape[0]
    per = outs[0].shape[0] // high
    for chunk in range(CORES * spots):
        half, rest = chunk // spots, chunk % spots
        out_ref = outs[chunk // per]
        start = (chunk % per) * high
        slot = lax.rem(rest - spot + spots, spots)
        side = jnp.where(core == half, 0, 1)
        for at, in_ref in enumerate(ins):

            @pl.when(side * spots + slot == at)
            def _():
                out_ref[start : start + high, :] = in_ref[...].astype(F32)


def spread(parts, place, width):
    whole = pl.BlockSpec(memory_space=pltpu.VMEM)
    return pl.pallas_call(
        functools.partial(spread_kernel, len(parts) // 2),
        out_shape=(jax.ShapeDtypeStruct((width, width), F32),) * 4,
        in_specs=[pl.BlockSpec(memory_space=pltpu.SMEM)] + [whole] * len(parts),
        out_specs=(whole,) * 4,
        compiler_params=pltpu.CompilerParams(vmem_limit_bytes=32 * 1024 * 1024),
    )(place, *parts)


def mask_bias(block_lists, rows):
    heads, blocks, listed = block_lists.shape
    names = jnp.arange(blocks, dtype=jnp.int32)
    allowed = jnp.any(block_lists[:, :, :, None] == names[None, None, None, :], axis=2)
    bias = jnp.where(jnp.swapaxes(allowed, 1, 2), 0.0, -1e30).astype(F32)
    return jnp.repeat(bias, rows // blocks, axis=2)


def swap_core(item, lon):
    return lax.ppermute(item, "lon", [(i, i ^ 1) for i in range(lon)])


def shift_chip(item, lon, by):
    return lax.ppermute(item, "lon", [(i, (i + by * CORES) % lon) for i in range(lon)])


def per_device(features, grad_out, w_query, w_key, w_value, w_out, block_lists):
    lat_rows, lon_cols, width = features.shape
    lat, lon = lax.axis_size("lat"), lax.axis_size("lon")
    spots = lon // CORES
    norm = 1.0 / math.sqrt(lat_rows * lon_cols * lat * lon)
    index = lax.axis_index("lon")
    place = jnp.stack([lax.rem(index, CORES), index // CORES]).astype(jnp.int32)
    w = jnp.concatenate([w_query, w_key, w_value], axis=1)
    bias = mask_bias(block_lists, lat * lat_rows)

    tiles = jnp.stack([features, grad_out]).transpose(2, 0, 1, 3)
    xg = lax.all_to_all(tiles, "lat", 0, 0, tiled=True)
    og, mine, send = column_pass(xg, w, w.T, w_out, w_out.T, bias, place, norm, spots)
    back = lax.all_to_all(og, "lat", 0, 0, tiled=True)
    taken = swap_core(send, lon)
    others = [shift_chip(mine[k] + taken[k], lon, k) for k in range(1, spots)]
    total = settle(back, mine, taken, others, lat)
    back = back.transpose(1, 2, 0, 3)
    total = jnp.sum(lax.all_to_all(total, "lat", 0, 0, tiled=True), axis=0)
    total = jnp.broadcast_to(total.astype(BF16)[None], (lat,) + total.shape)
    own = lax.all_to_all(total, "lat", 0, 0, tiled=True).reshape(-1, width)
    near = [own] + [shift_chip(own, lon, spots - k) for k in range(1, spots)]
    far = [swap_core(item, lon) for item in near]
    grads = spread(near + far, place, width)
    return (back[0], back[1]) + tuple(grads)


def solution(mesh):
    tile = P(("member", "lat"), "lon", None)
    in_specs = (tile, tile, P(), P(), P(), P(), P())
    out_specs = (tile, tile) + (P("member", None),) * 4
    return jax.shard_map(
        per_device, mesh=mesh, in_specs=in_specs, out_specs=out_specs, check_vma=False
    )
```

```python
import functools
import math

import jax
import jax.numpy as jnp
from jax import lax
from jax.experimental import pallas as pl
from jax.experimental.pallas import tpu as pltpu
from jax.sharding import PartitionSpec as P

HEADS = 8
BLK = 64
CORES = 2
BF16 = jnp.bfloat16
F32 = jnp.float32
NT = (((1,), (1,)), ((), ()))


def dot(left, right):
    return jnp.dot(left, right, preferred_element_type=F32)


def dot_nt(left, right):
    return lax.dot_general(left, right, NT, preferred_element_type=F32)


def forward_kernel(
    x_ref,
    w_ref,
    wt_ref,
    wo_ref,
    bias_ref,
    out_ref,
    probs_ref,
    rows_ref,
    kt_ref,
    xt_ref,
    att_ref,
    qt_ref,
    vt_ref,
):
    rows = probs_ref.shape[1]
    width = xt_ref.shape[0]
    head_dim = width // HEADS
    pair = 2 * head_dim
    scale = math.log2(math.e) / math.sqrt(head_dim)
    p = pl.program_id(0)

    @pl.when(p == 0)
    def _():
        x = x_ref[...].reshape(rows, width)
        xt_ref[...] = x.T
        for part, col_ref in enumerate((qt_ref, kt_ref, vt_ref)):
            span = slice(part * width, (part + 1) * width)
            rows_ref[:, span] = dot(x, w_ref[:, span]).astype(BF16)
            col_ref[...] = dot_nt(wt_ref[span, :], x).astype(BF16)

    blank = jnp.zeros((head_dim, rows), BF16)
    at = pl.multiple_of(p * pair, pair)
    k_pair = rows_ref[:, pl.ds(pl.multiple_of(width + at, pair), pair)]
    for odd in range(2):
        here = pl.multiple_of(at + odd * head_dim, head_dim)
        qt = qt_ref[pl.ds(here, head_dim), :]
        q_wide = jnp.concatenate([blank, qt] if odd else [qt, blank], axis=0)
        bias = bias_ref[2 * p + odd]
        scores = dot(k_pair, q_wide).reshape(rows // BLK, BLK, rows) + bias[:, None, :]
        scores = scores.reshape(rows, rows)
        top = jnp.max(scores, axis=0, keepdims=True)
        expo = jnp.exp2((scores - top) * scale)
        probs = expo * (1.0 / jnp.sum(expo, axis=0, keepdims=True))
        probs_ref[odd] = probs
        low = probs.astype(BF16)
        att_ref[pl.ds(here, head_dim), :] = dot(vt_ref[pl.ds(here, head_dim), :], low).astype(BF16)

    @pl.when(p == HEADS // 2 - 1)
    def _():
        x = x_ref[...].reshape(rows, width)
        output = x.astype(F32) + dot(att_ref[...].T, wo_ref[...])
        out_ref[...] = output.astype(BF16).reshape(out_ref.shape)


def forward_pass(x, w, wt, wo, bias):
    lat, lat_rows, width = x.shape
    rows = lat * lat_rows

    def whole(*shape):
        return pl.BlockSpec(shape, lambda p: (0,) * len(shape))

    return pl.pallas_call(
        forward_kernel,
        grid=(HEADS // 2,),
        out_shape=(
            jax.ShapeDtypeStruct(x.shape, BF16),
            jax.ShapeDtypeStruct((HEADS, rows, rows), F32),
            jax.ShapeDtypeStruct((rows, 3 * width), BF16),
            jax.ShapeDtypeStruct((width, rows), BF16),
            jax.ShapeDtypeStruct((width, rows), BF16),
            jax.ShapeDtypeStruct((width, rows), BF16),
        ),
        in_specs=[
            whole(*x.shape),
            whole(*w.shape),
            whole(*wt.shape),
            whole(*wo.shape),
            whole(*bias.shape),
        ],
        out_specs=(
            whole(*x.shape),
            pl.BlockSpec((2, rows, rows), lambda p: (p, 0, 0)),
            whole(rows, 3 * width),
            whole(width, rows),
            whole(width, rows),
            whole(width, rows),
        ),
        scratch_shapes=[pltpu.VMEM((width, rows), BF16)] * 2,
        compiler_params=pltpu.CompilerParams(vmem_limit_bytes=48 * 1024 * 1024),
        cost_estimate=pl.CostEstimate(
            flops=30 * rows * rows * width, bytes_accessed=16 << 20, transcendentals=HEADS * rows * rows
        ),
    )(x, w, wt, wo, bias)


def backward_kernel(
    norm,
    spots,
    place_ref,
    g_ref,
    probs_ref,
    q_ref,
    v_ref,
    kt_ref,
    xt_ref,
    att_ref,
    wo_ref,
    wot_ref,
    mine_ref,
    send_ref,
    right_ref,
    ga_ref,
    gat_ref,
    dqt_ref,
):
    rows, width = ga_ref.shape
    head_dim = width // HEADS
    pair = 2 * head_dim
    factor = 1.0 / math.sqrt(head_dim)
    p = pl.program_id(0)

    @pl.when(p == 0)
    def _():
        g = g_ref[...].reshape(rows, width)
        right_ref[3] = g
        ga_ref[...] = dot(g, wot_ref[...]).astype(BF16)
        gat_ref[...] = dot_nt(wo_ref[...], g).astype(BF16)

    first = lax.broadcasted_iota(jnp.int32, (rows, pair), 1) < head_dim
    blank = jnp.zeros((head_dim, rows), BF16)
    at = pl.multiple_of(p * pair, pair)
    g_pair = ga_ref[:, pl.ds(at, pair)]
    dvs, dks = [], []
    for odd in range(2):
        here = pl.multiple_of(at + odd * head_dim, head_dim)
        gt = gat_ref[pl.ds(here, head_dim), :]
        g_wide = jnp.concatenate([blank, gt] if odd else [gt, blank], axis=0)
        probs = probs_ref[odd]
        dvs.append(dot(probs.astype(BF16), g_pair))
        dprobs = dot(v_ref[...], g_wide)
        delta = jnp.sum(probs * dprobs, axis=0, keepdims=True)
        dscores = (probs * (dprobs - delta) * factor).astype(BF16)
        kt = kt_ref[odd * head_dim : (odd + 1) * head_dim, :]
        dqt_ref[pl.ds(here, head_dim), :] = dot(kt, dscores).astype(BF16)
        dks.append(dot(dscores, q_ref[...]))
    right_ref[1, :, pl.ds(at, pair)] = jnp.where(first, dks[0], dks[1]).astype(BF16)
    right_ref[2, :, pl.ds(at, pair)] = jnp.where(first, dvs[0], dvs[1]).astype(BF16)

    @pl.when(p == HEADS // 2 - 1)
    def _():
        right_ref[0] = dqt_ref[...].T
        core, spot = place_ref[0], place_ref[1]
        high = mine_ref.shape[1]
        per = width // high

        def grad_step(slot, carry):
            chunk = lax.rem(spot + slot, spots)
            start = pl.multiple_of(lax.rem(chunk, per) * high, high)
            for half, out_ref in enumerate((mine_ref, send_ref)):
                which = lax.rem(core + half, 2) * (spots // per) + chunk // per

                @pl.when(which < 3)
                def _():
                    lhs = xt_ref[pl.ds(start, high), :]
                    out_ref[slot] = dot(lhs, right_ref[which]) * norm

                @pl.when(which == 3)
                def _():
                    lhs = att_ref[pl.ds(start, high), :]
                    out_ref[slot] = dot(lhs, right_ref[which]) * norm

            return carry

        lax.fori_loop(0, spots, grad_step, 0)


def backward_pass(place, g, probs, qkv, kt, xt, att, wo, wot, norm, spots):
    lat, lat_rows, width = g.shape
    rows = lat * lat_rows
    pair = 2 * width // HEADS
    high = 4 * width // CORES // spots

    def whole(*shape):
        return pl.BlockSpec(shape, lambda p: (0,) * len(shape))

    return pl.pallas_call(
        functools.partial(backward_kernel, norm, spots),
        grid=(HEADS // 2,),
        out_shape=(
            jax.ShapeDtypeStruct((spots, high, width), F32),
            jax.ShapeDtypeStruct((spots, high, width), F32),
            jax.ShapeDtypeStruct((4, rows, width), BF16),
        ),
        in_specs=[
            pl.BlockSpec(memory_space=pltpu.SMEM),
            whole(*g.shape),
            pl.BlockSpec((2, rows, rows), lambda p: (p, 0, 0)),
            pl.BlockSpec((rows, pair), lambda p: (0, p)),
            pl.BlockSpec((rows, pair), lambda p: (0, HEADS + p)),
            pl.BlockSpec((pair, rows), lambda p: (p, 0)),
            whole(*xt.shape),
            whole(*att.shape),
            whole(*wo.shape),
            whole(*wot.shape),
        ],
        out_specs=(
            whole(spots, high, width),
            whole(spots, high, width),
            whole(4, rows, width),
        ),
        scratch_shapes=[
            pltpu.VMEM((rows, width), BF16),
            pltpu.VMEM((width, rows), BF16),
            pltpu.VMEM((width, rows), BF16),
        ],
        compiler_params=pltpu.CompilerParams(vmem_limit_bytes=48 * 1024 * 1024),
        cost_estimate=pl.CostEstimate(
            flops=30 * rows * rows * width, bytes_accessed=16 << 20, transcendentals=0
        ),
    )(place, g, probs, qkv, qkv, kt, xt, att, wo, wot)


def input_grad_kernel(right_ref, wt_ref, out_ref):
    width = wt_ref.shape[1]
    grad_in = right_ref[3].astype(F32) + dot(right_ref[0], wt_ref[:width, :])
    grad_in = grad_in + dot(right_ref[1], wt_ref[width : 2 * width, :])
    grad_in = grad_in + dot(right_ref[2], wt_ref[2 * width :, :])
    out_ref[...] = grad_in.astype(BF16).reshape(out_ref.shape)


def input_grad(right, wt, shape):
    _, rows, width = right.shape
    whole = pl.BlockSpec(memory_space=pltpu.VMEM)
    return pl.pallas_call(
        input_grad_kernel,
        out_shape=jax.ShapeDtypeStruct(shape, BF16),
        in_specs=[whole] * 2,
        out_specs=whole,
        compiler_params=pltpu.CompilerParams(vmem_limit_bytes=32 * 1024 * 1024),
        cost_estimate=pl.CostEstimate(
            flops=6 * rows * width * width, bytes_accessed=4 << 20, transcendentals=0
        ),
    )(right, wt)


def settle_kernel(output_ref, grad_in_ref, mine_ref, taken_ref, *refs):
    others, out_ref = refs[:-1], refs[-1]
    total = mine_ref[0] + taken_ref[0]
    for other_ref in others:
        total = total + other_ref[...]
    out_ref[...] = total.reshape(out_ref.shape)


def settle(output, grad_in, mine, taken, others, lat):
    _, high, width = mine.shape
    slot = pl.BlockSpec((1, high, width), lambda i: (0, 0, 0))
    chunk = pl.BlockSpec((high, width), lambda i: (0, 0))
    shape = (lat, high // lat, width)
    return pl.pallas_call(
        settle_kernel,
        grid=(1,),
        out_shape=jax.ShapeDtypeStruct(shape, F32),
        in_specs=[pl.BlockSpec(memory_space=pl.ANY)] * 2 + [slot, slot] + [chunk] * len(others),
        out_specs=pl.BlockSpec(shape, lambda i: (0, 0, 0)),
        compiler_params=pltpu.CompilerParams(vmem_limit_bytes=32 * 1024 * 1024),
    )(output, grad_in, mine, taken, *others)


def spread_kernel(spots, place_ref, *refs):
    ins, outs = refs[: 2 * spots], refs[2 * spots :]
    core, spot = place_ref[0], place_ref[1]
    high = ins[0].shape[0]
    per = outs[0].shape[0] // high
    for chunk in range(CORES * spots):
        half, rest = chunk // spots, chunk % spots
        out_ref = outs[chunk // per]
        start = (chunk % per) * high
        slot = lax.rem(rest - spot + spots, spots)
        side = jnp.where(core == half, 0, 1)
        for at, in_ref in enumerate(ins):

            @pl.when(side * spots + slot == at)
            def _():
                out_ref[start : start + high, :] = in_ref[...].astype(F32)


def spread(parts, place, width):
    whole = pl.BlockSpec(memory_space=pltpu.VMEM)
    return pl.pallas_call(
        functools.partial(spread_kernel, len(parts) // 2),
        out_shape=(jax.ShapeDtypeStruct((width, width), F32),) * 4,
        in_specs=[pl.BlockSpec(memory_space=pltpu.SMEM)] + [whole] * len(parts),
        out_specs=(whole,) * 4,
        compiler_params=pltpu.CompilerParams(vmem_limit_bytes=32 * 1024 * 1024),
    )(place, *parts)


def mask_bias(block_lists, rows):
    heads, blocks, listed = block_lists.shape
    names = jnp.arange(blocks, dtype=jnp.int32)
    allowed = jnp.any(block_lists[:, :, :, None] == names[None, None, None, :], axis=2)
    bias = jnp.where(jnp.swapaxes(allowed, 1, 2), 0.0, -1e30).astype(F32)
    return jnp.repeat(bias, rows // blocks, axis=2)


def swap_core(item, lon):
    return lax.ppermute(item, "lon", [(i, i ^ 1) for i in range(lon)])


def shift_chip(item, lon, by):
    return lax.ppermute(item, "lon", [(i, (i + by * CORES) % lon) for i in range(lon)])


def per_device(features, grad_out, w_query, w_key, w_value, w_out, block_lists):
    lat_rows, lon_cols, width = features.shape
    lat, lon = lax.axis_size("lat"), lax.axis_size("lon")
    spots = lon // CORES
    norm = 1.0 / math.sqrt(lat_rows * lon_cols * lat * lon)
    index = lax.axis_index("lon")
    place = jnp.stack([lax.rem(index, CORES), index // CORES]).astype(jnp.int32)
    w = jnp.concatenate([w_query, w_key, w_value], axis=1)
    bias = mask_bias(block_lists, lat * lat_rows)

    x = lax.all_to_all(features.transpose(1, 0, 2), "lat", 0, 0, tiled=True)
    g = lax.all_to_all(grad_out.transpose(1, 0, 2), "lat", 0, 0, tiled=True)
    wt = w.T
    output, probs, qkv, kt, xt, att = forward_pass(x, w, wt, w_out, bias)
    output = lax.all_to_all(output, "lat", 0, 0, tiled=True)
    mine, send, right = backward_pass(
        place, g, probs, qkv, kt, xt, att, w_out, w_out.T, norm, spots
    )
    grad_in = input_grad(right, wt, g.shape)

    taken = swap_core(send, lon)
    others = [shift_chip(mine[k] + taken[k], lon, k) for k in range(1, spots)]
    total = settle(output, grad_in, mine, taken, others, lat)
    total = jnp.sum(lax.all_to_all(total, "lat", 0, 0, tiled=True), axis=0)
    total = jnp.broadcast_to(total.astype(BF16)[None], (lat,) + total.shape)
    own = lax.all_to_all(total, "lat", 0, 0, tiled=True).reshape(-1, width)
    grad_in = lax.all_to_all(grad_in, "lat", 0, 0, tiled=True)
    near = [own] + [shift_chip(own, lon, spots - k) for k in range(1, spots)]
    far = [swap_core(item, lon) for item in near]
    grads = spread(near + far, place, width)
    return (output.transpose(1, 0, 2), grad_in.transpose(1, 0, 2)) + tuple(grads)


def solution(mesh):
    tile = P(("member", "lat"), "lon", None)
    in_specs = (tile, tile, P(), P(), P(), P(), P())
    out_specs = (tile, tile) + (P("member", None),) * 4
    return jax.shard_map(
        per_device, mesh=mesh, in_specs=in_specs, out_specs=out_specs, check_vma=False
    )
```

```python
import functools
import math

import jax
import jax.numpy as jnp
from jax import lax
from jax.experimental import pallas as pl
from jax.experimental.pallas import tpu as pltpu
from jax.sharding import PartitionSpec as P

HEADS = 8
BLK = 64
CORES = 2
BF16 = jnp.bfloat16
F32 = jnp.float32
NT = (((1,), (1,)), ((), ()))


def dot(left, right):
    return jnp.dot(left, right, preferred_element_type=F32)


def dot_nt(left, right):
    return lax.dot_general(left, right, NT, preferred_element_type=F32)


def column_kernel(
    norm,
    spots,
    place_ref,
    xg_ref,
    w_ref,
    wt_ref,
    wo_ref,
    bias_ref,
    *refs,
):
    og_out, grad_outs = refs[0], refs[1 : 1 + 2 * spots]
    rows_ref, cols_ref, ga_ref, gat_ref, left_ref, right_ref, dqt_ref = refs[1 + 2 * spots : -4]
    og_ref, grad_ref, og_sem, grad_sem = refs[-4:]
    rows, width = ga_ref.shape
    head_dim = width // HEADS
    pair = 2 * head_dim
    factor = 1.0 / math.sqrt(head_dim)
    scale = factor * math.log2(math.e)
    x = xg_ref[:, 0].reshape(rows, width)
    g = xg_ref[:, 1].reshape(rows, width)
    left_ref[0] = x.T
    right_ref[3] = g

    for part in range(3):
        span = slice(part * width, (part + 1) * width)
        rows_ref[:, span] = dot(x, w_ref[:, span]).astype(BF16)
        cols_ref[span, :] = dot_nt(wt_ref[span, :], x).astype(BF16)
    ga_ref[...] = dot_nt(g, wo_ref[...]).astype(BF16)
    gat_ref[...] = dot_nt(wo_ref[...], g).astype(BF16)

    first = lax.broadcasted_iota(jnp.int32, (rows, pair), 1) < head_dim
    blank = jnp.zeros((head_dim, rows), BF16)

    def pair_step(p, carry):
        at = pl.multiple_of(p * pair, pair)
        q_pair = rows_ref[:, pl.ds(at, pair)]
        k_pair = rows_ref[:, pl.ds(pl.multiple_of(width + at, pair), pair)]
        v_pair = rows_ref[:, pl.ds(pl.multiple_of(2 * width + at, pair), pair)]
        g_pair = ga_ref[:, pl.ds(at, pair)]
        dvs, dks = [], []
        for odd in range(2):
            here = pl.multiple_of(at + odd * head_dim, head_dim)
            qt = cols_ref[pl.ds(here, head_dim), :]
            kt = cols_ref[pl.ds(pl.multiple_of(width + here, head_dim), head_dim), :]
            vt = cols_ref[pl.ds(pl.multiple_of(2 * width + here, head_dim), head_dim), :]
            gt = gat_ref[pl.ds(here, head_dim), :]
            q_wide = jnp.concatenate([blank, qt] if odd else [qt, blank], axis=0)
            g_wide = jnp.concatenate([blank, gt] if odd else [gt, blank], axis=0)
            bias = bias_ref[2 * p + odd]
            scores = dot(k_pair, q_wide).reshape(rows // BLK, BLK, rows) + bias[:, None, :]
            scores = scores.reshape(rows, rows)
            top = jnp.max(scores, axis=0, keepdims=True)
            expo = jnp.exp2((scores - top) * scale)
            probs = expo * (1.0 / jnp.sum(expo, axis=0, keepdims=True))
            low = probs.astype(BF16)
            left_ref[1, pl.ds(here, head_dim), :] = dot(vt, low).astype(BF16)
            dvs.append(dot(low, g_pair))
            dprobs = dot(v_pair, g_wide)
            delta = jnp.sum(probs * dprobs, axis=0, keepdims=True)
            dscores = (probs * (dprobs - delta) * factor).astype(BF16)
            dqt_ref[pl.ds(here, head_dim), :] = dot(kt, dscores).astype(BF16)
            dks.append(dot(dscores, q_pair))
        right_ref[1, :, pl.ds(at, pair)] = jnp.where(first, dks[0], dks[1]).astype(BF16)
        right_ref[2, :, pl.ds(at, pair)] = jnp.where(first, dvs[0], dvs[1]).astype(BF16)
        return carry

    lax.fori_loop(0, HEADS // 2, pair_step, 0, unroll=True)
    right_ref[0] = dqt_ref[...].T
    core, spot = place_ref[0], place_ref[1]
    high = grad_ref.shape[2]
    per = width // high
    copies = []
    for half in (1, 0):
        for slot in list(range(1, spots)) + [0]:
            chunk = lax.rem(spot + slot, spots)
            which = lax.rem(core + half, 2) * (spots // per) + chunk // per
            start = pl.multiple_of(lax.rem(chunk, per) * high, high)
            lhs = left_ref[which // 3, pl.ds(start, high), :]
            grad_ref[half, slot] = dot(lhs, right_ref[which]) * norm
            at = half * spots + slot
            copy = pltpu.make_async_copy(grad_ref.at[half, slot], grad_outs[at], grad_sem.at[at])
            copy.start()
            copies.append(copy)

    attended = left_ref[1].T
    output = x.astype(F32) + dot(attended, wo_ref[...])
    og_ref[:, 0] = output.astype(BF16).reshape(og_ref.shape[0], og_ref.shape[2], width)
    grad_in = g.astype(F32) + dot(right_ref[0], wt_ref[:width, :])
    grad_in = grad_in + dot(right_ref[1], wt_ref[width : 2 * width, :])
    grad_in = grad_in + dot(right_ref[2], wt_ref[2 * width :, :])
    og_ref[:, 1] = grad_in.astype(BF16).reshape(og_ref.shape[0], og_ref.shape[2], width)
    copy = pltpu.make_async_copy(og_ref, og_out, og_sem)
    copy.start()
    for item in copies + [copy]:
        item.wait()


def column_pass(xg, w, wt, wo, bias, place, norm, spots):
    lat, _, lat_rows, width = xg.shape
    rows = lat * lat_rows
    high = 4 * width // CORES // spots
    whole = pl.BlockSpec(memory_space=pltpu.VMEM)
    return pl.pallas_call(
        functools.partial(column_kernel, norm, spots),
        out_shape=(jax.ShapeDtypeStruct(xg.shape, BF16),)
        + (jax.ShapeDtypeStruct((high, width), F32),) * (2 * spots),
        in_specs=[pl.BlockSpec(memory_space=pltpu.SMEM)] + [whole] * 5,
        out_specs=(pl.BlockSpec(memory_space=pltpu.HBM),) * (1 + 2 * spots),
        scratch_shapes=[
            pltpu.VMEM((rows, 3 * width), BF16),
            pltpu.VMEM((3 * width, rows), BF16),
            pltpu.VMEM((rows, width), BF16),
            pltpu.VMEM((width, rows), BF16),
            pltpu.VMEM((2, width, rows), BF16),
            pltpu.VMEM((4, rows, width), BF16),
            pltpu.VMEM((width, rows), BF16),
            pltpu.VMEM(xg.shape, BF16),
            pltpu.VMEM((2, spots, high, width), F32),
            pltpu.SemaphoreType.DMA,
            pltpu.SemaphoreType.DMA((2 * spots,)),
        ],
        compiler_params=pltpu.CompilerParams(vmem_limit_bytes=48 * 1024 * 1024),
    )(place, xg, w, wt, wo, bias)


def settle_kernel(back_ref, *refs):
    total = refs[0][...]
    for other_ref in refs[1:-1]:
        total = total + other_ref[...]
    refs[-1][...] = total.reshape(refs[-1].shape)


def settle(back, parts, lat):
    high, width = parts[0].shape
    chunk = pl.BlockSpec((high, width), lambda i: (0, 0))
    shape = (lat, high // lat, width)
    return pl.pallas_call(
        settle_kernel,
        grid=(1,),
        out_shape=jax.ShapeDtypeStruct(shape, F32),
        in_specs=[pl.BlockSpec(memory_space=pl.ANY)] + [chunk] * len(parts),
        out_specs=pl.BlockSpec(shape, lambda i: (0, 0, 0)),
        compiler_params=pltpu.CompilerParams(vmem_limit_bytes=32 * 1024 * 1024),
    )(back, *parts)


def spread_kernel(far, spots, place_ref, *refs):
    ins = refs[:spots]
    outs = refs[-6:-2]
    wide_ref, sem = refs[-2:]
    core, spot = place_ref[0], place_ref[1]
    high = wide_ref.shape[1]
    per = outs[0].shape[0] // high
    for slot, in_ref in enumerate(ins):
        wide_ref[slot] = in_ref[...].astype(F32)
    for half in range(CORES):

        @pl.when(lax.rem(core + far, CORES) == half)
        def _():
            copies = []
            for rest in range(spots):
                chunk = half * spots + rest
                start = (chunk % per) * high
                slot = lax.rem(rest - spot + spots, spots)
                copy = pltpu.make_async_copy(
                    wide_ref.at[slot],
                    outs[chunk // per].at[pl.ds(start, high), :],
                    sem.at[rest],
                )
                copy.start()
                copies.append(copy)
            for copy in copies:
                copy.wait()


def spread(parts, place, width, held=None):
    spots = len(parts)
    whole = pl.BlockSpec(memory_space=pltpu.VMEM)
    there = pl.BlockSpec(memory_space=pltpu.HBM)
    held = () if held is None else held
    return pl.pallas_call(
        functools.partial(spread_kernel, 1 if held else 0, spots),
        out_shape=(jax.ShapeDtypeStruct((width, width), F32),) * 4,
        in_specs=[pl.BlockSpec(memory_space=pltpu.SMEM)] + [whole] * spots + [there] * len(held),
        out_specs=(there,) * 4,
        input_output_aliases={1 + spots + i: i for i in range(len(held))},
        scratch_shapes=[
            pltpu.VMEM((spots,) + parts[0].shape, F32),
            pltpu.SemaphoreType.DMA((spots,)),
        ],
        compiler_params=pltpu.CompilerParams(vmem_limit_bytes=32 * 1024 * 1024),
        cost_estimate=pl.CostEstimate(flops=0, bytes_accessed=4 << 20, transcendentals=0),
    )(place, *parts, *held)


def mask_bias(block_lists, rows):
    heads, blocks, listed = block_lists.shape
    names = jnp.arange(blocks, dtype=jnp.int32)
    allowed = jnp.any(block_lists[:, :, :, None] == names[None, None, None, :], axis=2)
    bias = jnp.where(jnp.swapaxes(allowed, 1, 2), 0.0, -1e30).astype(F32)
    return jnp.repeat(bias, rows // blocks, axis=2)


def swap_core(item, lon):
    return lax.ppermute(item, "lon", [(i, i ^ 1) for i in range(lon)])


def shift_chip(item, lon, by):
    return lax.ppermute(item, "lon", [(i, (i + by * CORES) % lon) for i in range(lon)])


def per_device(features, grad_out, w_query, w_key, w_value, w_out, block_lists):
    lat_rows, lon_cols, width = features.shape
    lat, lon = lax.axis_size("lat"), lax.axis_size("lon")
    spots = lon // CORES
    norm = 1.0 / math.sqrt(lat_rows * lon_cols * lat * lon)
    index = lax.axis_index("lon")
    place = jnp.stack([lax.rem(index, CORES), index // CORES]).astype(jnp.int32)
    w = jnp.concatenate([w_query, w_key, w_value], axis=1)
    bias = mask_bias(block_lists, lat * lat_rows)

    tiles = jnp.stack([features, grad_out]).transpose(2, 0, 1, 3)
    xg = lax.all_to_all(tiles, "lat", 0, 0, tiled=True)
    og, *parts = column_pass(xg, w, w.T, w_out, bias, place, norm, spots)
    mine, send = parts[:spots], parts[spots:]
    back = lax.all_to_all(og, "lat", 0, 0, tiled=True)
    others = [
        shift_chip(mine[k] + swap_core(send[k], lon), lon, k) for k in range(1, spots)
    ]
    total = settle(back, [mine[0], swap_core(send[0], lon)] + others, lat)
    back = back.transpose(1, 2, 0, 3)
    total = jnp.sum(lax.all_to_all(total, "lat", 0, 0, tiled=True), axis=0)
    total = jnp.broadcast_to(total.astype(BF16)[None], (lat,) + total.shape)
    own = lax.all_to_all(total, "lat", 0, 0, tiled=True).reshape(-1, width)
    near = [own] + [shift_chip(own, lon, spots - k) for k in range(1, spots)]
    far = [swap_core(item, lon) for item in near]
    grads = spread(far, place, width, spread(near, place, width))
    return (back[0], back[1]) + tuple(grads)


def solution(mesh):
    tile = P(("member", "lat"), "lon", None)
    in_specs = (tile, tile, P(), P(), P(), P(), P())
    out_specs = (tile, tile) + (P("member", None),) * 4
    return jax.shard_map(
        per_device, mesh=mesh, in_specs=in_specs, out_specs=out_specs, check_vma=False
    )
```

```python
import functools
import math

import jax
import jax.numpy as jnp
from jax import lax
from jax.experimental import pallas as pl
from jax.experimental.pallas import tpu as pltpu
from jax.sharding import PartitionSpec as P

HEADS = 8
BLK = 64
CORES = 2
BF16 = jnp.bfloat16
F32 = jnp.float32
NT = (((1,), (1,)), ((), ()))


def dot(left, right):
    return jnp.dot(left, right, preferred_element_type=F32)


def dot_nt(left, right):
    return lax.dot_general(left, right, NT, preferred_element_type=F32)


def column_kernel(
    norm,
    spots,
    place_ref,
    xg_ref,
    w_ref,
    wt_ref,
    wo_ref,
    lists_ref,
    *refs,
):
    og_out, grad_outs = refs[0], refs[1 : 1 + 2 * spots]
    rows_ref, cols_ref, ga_ref, gat_ref, left_ref, right_ref, dqt_ref = refs[1 + 2 * spots : 8 + 2 * spots]
    kd_ref, vd_ref, kt_ref, vt_ref, *acc_refs = refs[8 + 2 * spots : -4]
    og_ref, grad_ref, og_sem, grad_sem = refs[-4:]
    rows, width = ga_ref.shape
    head_dim = width // HEADS
    pair = 2 * head_dim
    factor = 1.0 / math.sqrt(head_dim)
    scale = factor * math.log2(math.e)
    x = xg_ref[:, 0].reshape(rows, width)
    g = xg_ref[:, 1].reshape(rows, width)
    left_ref[0] = x.T
    right_ref[3] = g

    for part in range(3):
        span = slice(part * width, (part + 1) * width)
        rows_ref[:, span] = dot(x, w_ref[:, span]).astype(BF16)
        cols_ref[span, :] = dot_nt(wt_ref[span, :], x).astype(BF16)
    ga_ref[...] = dot_nt(g, wo_ref[...]).astype(BF16)
    gat_ref[...] = dot_nt(wo_ref[...], g).astype(BF16)

    blocks, listed = lists_ref.shape[1:]
    side = listed * BLK
    group = side // head_dim
    low = lax.broadcasted_iota(jnp.int32, (BLK, pair), 1) < head_dim
    low_rows = lax.broadcasted_iota(jnp.int32, (rows, pair), 1) < head_dim
    low_side = lax.broadcasted_iota(jnp.int32, (side, pair), 1) < head_dim
    own = (
        lax.broadcasted_iota(jnp.int32, (side, side), 0) // head_dim
        == lax.broadcasted_iota(jnp.int32, (side, side), 1) // BLK
    )
    owner = lax.broadcasted_iota(jnp.int32, (head_dim, side), 1) // BLK
    nothing = jnp.zeros((side, side), BF16)

    def swapped(tile):
        return jnp.concatenate([tile[:, head_dim:], tile[:, :head_dim]], axis=1)

    for tile in range(width // pair):
        span = slice(tile * pair, (tile + 1) * pair)
        for at, dup_ref in enumerate((kd_ref, vd_ref)):
            straight = rows_ref[:, (at + 1) * width + tile * pair :][:, :pair]
            crossed = swapped(straight)
            dup_ref[2 * tile] = jnp.where(low_rows, straight, crossed)
            dup_ref[2 * tile + 1] = jnp.where(low_rows, crossed, straight)
        for at, turn_ref in enumerate((kt_ref, vt_ref)):
            straight = cols_ref[(at + 1) * width : (at + 2) * width, span]
            turn_ref[0, :, span] = straight
            turn_ref[1, :, span] = swapped(straight)

    def diagonal(stack):
        out = stack[:head_dim]
        for at in range(1, group):
            out = jnp.where(owner == at, stack[at * head_dim : (at + 1) * head_dim], out)
        return out

    def pair_step(p, carry):
        at = pl.multiple_of(p * pair, pair)
        totals = []
        for odd in range(2):
            head = 2 * p + odd
            here = pl.multiple_of(at + odd * head_dim, head_dim)
            accs = acc_refs[2 * odd : 2 * odd + 2]
            for acc_ref in accs:
                acc_ref[...] = jnp.zeros_like(acc_ref)
            for part in range(blocks // group):
                span = slice(part * side, (part + 1) * side)
                names = [
                    [lists_ref[head, part * group + a, k] for k in range(listed)]
                    for a in range(group)
                ]
                starts = [[pl.multiple_of(n * BLK, BLK) for n in row] for row in names]
                tiles = [[pl.multiple_of(n // 2 * pair, pair) for n in row] for row in names]

                def gathered(ref):
                    columns = []
                    for b in range(group // 2):
                        pieces = [
                            jnp.where(
                                low,
                                ref[head, pl.ds(starts[2 * b][k], BLK), :],
                                ref[head, pl.ds(starts[2 * b + 1][k], BLK), :],
                            )
                            for k in range(listed)
                        ]
                        columns.append(jnp.concatenate(pieces, axis=0))
                    return jnp.concatenate(columns, axis=1)

                def gathered_t(ref):
                    lines = []
                    for a in range(group):
                        pieces = []
                        for b in range(listed // 2):
                            even, other = names[a][2 * b], names[a][2 * b + 1]
                            pieces.append(
                                jnp.where(
                                    low,
                                    ref[
                                        lax.rem(even, 2),
                                        pl.ds(here, head_dim),
                                        pl.ds(tiles[a][2 * b], pair),
                                    ],
                                    ref[
                                        1 - lax.rem(other, 2),
                                        pl.ds(here, head_dim),
                                        pl.ds(tiles[a][2 * b + 1], pair),
                                    ],
                                )
                            )
                        lines.append(jnp.concatenate(pieces, axis=1))
                    return jnp.concatenate(lines, axis=0)

                def spaced_t(ref):
                    line = ref[pl.ds(here, head_dim), span]
                    return jnp.where(own, jnp.concatenate([line] * group, axis=0), nothing)

                def spaced(tile):
                    crossed = swapped(tile)
                    both = (crossed, tile) if odd else (tile, crossed)
                    line = jnp.where(low_side, *both)
                    return jnp.where(own, jnp.concatenate([line] * (group // 2), axis=1), nothing)

                scores = dot(gathered(kd_ref), spaced_t(cols_ref))
                top = jnp.max(scores, axis=0, keepdims=True)
                expo = jnp.exp2((scores - top) * scale)
                probs = expo * (1.0 / jnp.sum(expo, axis=0, keepdims=True))
                probs_low = probs.astype(BF16)
                attended = diagonal(dot(gathered_t(vt_ref), probs_low))
                left_ref[1, pl.ds(here, head_dim), span] = attended.astype(BF16)
                dprobs = dot(gathered(vd_ref), spaced_t(gat_ref))
                delta = jnp.sum(probs * dprobs, axis=0, keepdims=True)
                dscores = (probs * (dprobs - delta) * factor).astype(BF16)
                dquery = diagonal(dot(gathered_t(kt_ref), dscores))
                dqt_ref[pl.ds(here, head_dim), span] = dquery.astype(BF16)
                dvalues = dot(probs_low, spaced(ga_ref[span, pl.ds(at, pair)]))
                dkeys = dot(dscores, spaced(rows_ref[span, pl.ds(at, pair)]))
                for acc_ref, terms in zip(accs, (dkeys, dvalues)):
                    for k in range(listed):
                        for a in range(group):
                            piece = terms[k * BLK : (k + 1) * BLK, a // 2 * pair : (a // 2 + 1) * pair]
                            piece = jnp.where(low, 0.0, piece) if a % 2 else jnp.where(low, piece, 0.0)
                            acc_ref[pl.ds(starts[a][k], BLK), :] += piece
            totals.append([acc_ref[...] + swapped(acc_ref[...]) for acc_ref in accs])
        for which in range(2):
            both = jnp.where(low_rows, totals[0][which], totals[1][which])
            right_ref[1 + which, :, pl.ds(at, pair)] = both.astype(BF16)
        return carry

    lax.fori_loop(0, HEADS // 2, pair_step, 0, unroll=True)
    right_ref[0] = dqt_ref[...].T
    core, spot = place_ref[0], place_ref[1]
    high = grad_ref.shape[2]
    per = width // high
    copies = []
    for half in (1, 0):
        for slot in list(range(1, spots)) + [0]:
            chunk = lax.rem(spot + slot, spots)
            which = lax.rem(core + half, 2) * (spots // per) + chunk // per
            start = pl.multiple_of(lax.rem(chunk, per) * high, high)
            lhs = left_ref[which // 3, pl.ds(start, high), :]
            grad_ref[half, slot] = dot(lhs, right_ref[which]) * norm
            at = half * spots + slot
            copy = pltpu.make_async_copy(grad_ref.at[half, slot], grad_outs[at], grad_sem.at[at])
            copy.start()
            copies.append(copy)

    attended = left_ref[1].T
    output = x.astype(F32) + dot(attended, wo_ref[...])
    og_ref[0] = output.astype(BF16).reshape(og_ref.shape[1:])
    copies.append(pltpu.make_async_copy(og_ref.at[0], og_out.at[:, 0], og_sem.at[0]))
    copies[-1].start()
    grad_in = g.astype(F32) + dot(right_ref[0], wt_ref[:width, :])
    grad_in = grad_in + dot(right_ref[1], wt_ref[width : 2 * width, :])
    grad_in = grad_in + dot(right_ref[2], wt_ref[2 * width :, :])
    og_ref[1] = grad_in.astype(BF16).reshape(og_ref.shape[1:])
    copies.append(pltpu.make_async_copy(og_ref.at[1], og_out.at[:, 1], og_sem.at[1]))
    copies[-1].start()
    for copy in copies:
        copy.wait()


def column_pass(xg, w, wt, wo, lists, place, norm, spots):
    lat, _, lat_rows, width = xg.shape
    rows = lat * lat_rows
    high = 4 * width // CORES // spots
    whole = pl.BlockSpec(memory_space=pltpu.VMEM)
    return pl.pallas_call(
        functools.partial(column_kernel, norm, spots),
        out_shape=(jax.ShapeDtypeStruct(xg.shape, BF16),)
        + (jax.ShapeDtypeStruct((high, width), F32),) * (2 * spots),
        in_specs=[pl.BlockSpec(memory_space=pltpu.SMEM)]
        + [whole] * 4
        + [pl.BlockSpec(memory_space=pltpu.SMEM)],
        out_specs=(pl.BlockSpec(memory_space=pltpu.HBM),) * (1 + 2 * spots),
        scratch_shapes=[
            pltpu.VMEM((rows, 3 * width), BF16),
            pltpu.VMEM((3 * width, rows), BF16),
            pltpu.VMEM((rows, width), BF16),
            pltpu.VMEM((width, rows), BF16),
            pltpu.VMEM((2, width, rows), BF16),
            pltpu.VMEM((4, rows, width), BF16),
            pltpu.VMEM((width, rows), BF16),
            pltpu.VMEM((HEADS, rows, 2 * width // HEADS), BF16),
            pltpu.VMEM((HEADS, rows, 2 * width // HEADS), BF16),
            pltpu.VMEM((2, width, rows), BF16),
            pltpu.VMEM((2, width, rows), BF16),
            pltpu.VMEM((rows, 2 * width // HEADS), F32),
            pltpu.VMEM((rows, 2 * width // HEADS), F32),
            pltpu.VMEM((rows, 2 * width // HEADS), F32),
            pltpu.VMEM((rows, 2 * width // HEADS), F32),
            pltpu.VMEM((2, lat, lat_rows, width), BF16),
            pltpu.VMEM((2, spots, high, width), F32),
            pltpu.SemaphoreType.DMA((2,)),
            pltpu.SemaphoreType.DMA((2 * spots,)),
        ],
        compiler_params=pltpu.CompilerParams(vmem_limit_bytes=60 * 1024 * 1024),
    )(place, xg, w, wt, wo, lists)


def tiles_kernel(x_in, g_in, out, x_ref, g_ref, tile_ref, in_sem, out_sem):
    arrivals = []
    for at, (source, ref) in enumerate(((x_in, x_ref), (g_in, g_ref))):
        arrivals.append(pltpu.make_async_copy(source, ref, in_sem.at[at]))
        arrivals[-1].start()
    copies = []
    for at, ref in enumerate((x_ref, g_ref)):
        arrivals[at].wait()
        tile_ref[at] = jnp.swapaxes(ref[...], 0, 1)
        copies.append(pltpu.make_async_copy(tile_ref.at[at], out.at[:, at], out_sem.at[at]))
        copies[-1].start()
    for copy in copies:
        copy.wait()


def to_tiles(x, g):
    lat_rows, cols, width = x.shape
    there = pl.BlockSpec(memory_space=pltpu.HBM)
    return pl.pallas_call(
        tiles_kernel,
        out_shape=jax.ShapeDtypeStruct((cols, 2, lat_rows, width), BF16),
        in_specs=[there] * 2,
        out_specs=there,
        scratch_shapes=[
            pltpu.VMEM(x.shape, BF16),
            pltpu.VMEM(x.shape, BF16),
            pltpu.VMEM((2, cols, lat_rows, width), BF16),
            pltpu.SemaphoreType.DMA((2,)),
            pltpu.SemaphoreType.DMA((2,)),
        ],
        compiler_params=pltpu.CompilerParams(vmem_limit_bytes=60 * 1024 * 1024),
    )(x, g)


def settle_kernel(back_ref, *refs):
    total = refs[0][...]
    for other_ref in refs[1:-1]:
        total = total + other_ref[...]
    refs[-1][...] = total.reshape(refs[-1].shape)


def settle(back, parts, lat):
    high, width = parts[0].shape
    chunk = pl.BlockSpec((high, width), lambda i: (0, 0))
    shape = (lat, high // lat, width)
    return pl.pallas_call(
        settle_kernel,
        grid=(1,),
        out_shape=jax.ShapeDtypeStruct(shape, F32),
        in_specs=[pl.BlockSpec(memory_space=pl.ANY)] + [chunk] * len(parts),
        out_specs=pl.BlockSpec(shape, lambda i: (0, 0, 0)),
        compiler_params=pltpu.CompilerParams(vmem_limit_bytes=32 * 1024 * 1024),
    )(back, *parts)


def spread_kernel(spots, place_ref, *refs):
    ins, back_in = refs[: CORES * spots], refs[CORES * spots]
    outs, tile_outs = refs[CORES * spots + 1 : -8], refs[-8:-6]
    wide_ref, back_ref, tile_ref, sem, back_sem, tile_sem = refs[-6:]
    arrive = pltpu.make_async_copy(back_in, back_ref, back_sem)
    arrive.start()
    core, spot = place_ref[0], place_ref[1]
    high = wide_ref.shape[1]
    per = outs[0].shape[0] // high
    copies = []
    for at, in_ref in enumerate(ins):
        far, slot = at // spots, at % spots
        wide_ref[at] = in_ref[...].astype(F32)
        chunk = lax.rem(core + far, CORES) * spots + lax.rem(spot + slot, spots)
        start = pl.multiple_of(lax.rem(chunk, per) * high, high)
        for which, out_ref in enumerate(outs):
            there = out_ref.at[pl.ds(start, high), :]
            copy = pltpu.make_async_copy(wide_ref.at[at], there, sem.at[at])

            @pl.when(chunk // per == which)
            def _():
                copy.start()

        copies.append(copy)
    arrive.wait()
    for at, out_ref in enumerate(tile_outs):
        tile_ref[at] = jnp.swapaxes(back_ref[:, at], 0, 1)
        copy = pltpu.make_async_copy(tile_ref.at[at], out_ref, tile_sem.at[at])
        copy.start()
        copies.append(copy)
    for copy in copies:
        copy.wait()


def spread(parts, back, place, width):
    cols, _, lat_rows, _ = back.shape
    tile = (lat_rows, cols, width)
    whole = pl.BlockSpec(memory_space=pltpu.VMEM)
    there = pl.BlockSpec(memory_space=pltpu.HBM)
    return pl.pallas_call(
        functools.partial(spread_kernel, len(parts) // CORES),
        out_shape=(jax.ShapeDtypeStruct((width, width), F32),) * 4
        + (jax.ShapeDtypeStruct(tile, BF16),) * 2,
        in_specs=[pl.BlockSpec(memory_space=pltpu.SMEM)] + [whole] * len(parts) + [there],
        out_specs=(there,) * 6,
        scratch_shapes=[
            pltpu.VMEM((len(parts),) + parts[0].shape, F32),
            pltpu.VMEM(back.shape, BF16),
            pltpu.VMEM((2,) + tile, BF16),
            pltpu.SemaphoreType.DMA((len(parts),)),
            pltpu.SemaphoreType.DMA,
            pltpu.SemaphoreType.DMA((2,)),
        ],
        compiler_params=pltpu.CompilerParams(vmem_limit_bytes=32 * 1024 * 1024),
    )(place, *parts, back)


def swap_core(item, lon):
    return lax.ppermute(item, "lon", [(i, i ^ 1) for i in range(lon)])


def shift_chip(item, lon, by):
    return lax.ppermute(item, "lon", [(i, (i + by * CORES) % lon) for i in range(lon)])


def per_device(features, grad_out, w_query, w_key, w_value, w_out, block_lists):
    lat_rows, lon_cols, width = features.shape
    lat, lon = lax.axis_size("lat"), lax.axis_size("lon")
    spots = lon // CORES
    norm = 1.0 / math.sqrt(lat_rows * lon_cols * lat * lon)
    index = lax.axis_index("lon")
    place = jnp.stack([lax.rem(index, CORES), index // CORES]).astype(jnp.int32)
    w = jnp.concatenate([w_query, w_key, w_value], axis=1)

    xg = lax.all_to_all(to_tiles(features, grad_out), "lat", 0, 0, tiled=True)
    og, *parts = column_pass(xg, w, w.T, w_out, block_lists, place, norm, spots)
    mine, send = parts[:spots], parts[spots:]
    back = lax.all_to_all(og, "lat", 0, 0, tiled=True)
    others = [
        shift_chip(mine[k] + swap_core(send[k], lon), lon, k) for k in range(1, spots)
    ]
    total = settle(back, [mine[0], swap_core(send[0], lon)] + others, lat)
    total = jnp.sum(lax.all_to_all(total, "lat", 0, 0, tiled=True), axis=0)
    total = jnp.broadcast_to(total.astype(BF16)[None], (lat,) + total.shape)
    own = lax.all_to_all(total, "lat", 0, 0, tiled=True).reshape(-1, width)
    near = [own] + [shift_chip(own, lon, spots - k) for k in range(1, spots)]
    far = [swap_core(item, lon) for item in near]
    *grads, output, grad_in = spread(near + far, back, place, width)
    return (output, grad_in) + tuple(grads)


def solution(mesh):
    tile = P(("member", "lat"), "lon", None)
    in_specs = (tile, tile, P(), P(), P(), P(), P())
    out_specs = (tile, tile) + (P("member", None),) * 4
    return jax.shard_map(
        per_device, mesh=mesh, in_specs=in_specs, out_specs=out_specs, check_vma=False
    )
```

```python
import functools
import math

import jax
import jax.numpy as jnp
from jax import lax
from jax.experimental import pallas as pl
from jax.experimental.pallas import tpu as pltpu
from jax.sharding import PartitionSpec as P

HEADS = 8
BLK = 64
CORES = 2
BF16 = jnp.bfloat16
F32 = jnp.float32
NT = (((1,), (1,)), ((), ()))


def dot(left, right):
    return jnp.dot(left, right, preferred_element_type=F32)


def dot_nt(left, right):
    return lax.dot_general(left, right, NT, preferred_element_type=F32)


def column_kernel(
    norm,
    spots,
    place_ref,
    xg_ref,
    w_ref,
    wt_ref,
    wo_ref,
    lists_ref,
    *refs,
):
    og_out, grad_outs = refs[0], refs[1 : 1 + 2 * spots]
    rows_ref, cols_ref, ga_ref, gat_ref, left_ref, right_ref, dqt_ref = refs[1 + 2 * spots : 8 + 2 * spots]
    kd_ref, vd_ref, kt_ref, vt_ref, *acc_refs = refs[8 + 2 * spots : -4]
    og_ref, grad_ref, og_sem, grad_sem = refs[-4:]
    rows, width = ga_ref.shape
    head_dim = width // HEADS
    pair = 2 * head_dim
    factor = 1.0 / math.sqrt(head_dim)
    scale = factor * math.log2(math.e)
    x = xg_ref[:, 0].reshape(rows, width)
    g = xg_ref[:, 1].reshape(rows, width)
    left_ref[0] = x.T
    right_ref[3] = g

    for part in range(3):
        span = slice(part * width, (part + 1) * width)
        rows_ref[:, span] = dot(x, w_ref[:, span]).astype(BF16)
        cols_ref[span, :] = dot_nt(wt_ref[span, :], x).astype(BF16)
    ga_ref[...] = dot_nt(g, wo_ref[...]).astype(BF16)
    gat_ref[...] = dot_nt(wo_ref[...], g).astype(BF16)

    blocks, listed = lists_ref.shape[1:]
    side = listed * BLK
    group = side // head_dim
    low = lax.broadcasted_iota(jnp.int32, (BLK, pair), 1) < head_dim
    low_rows = lax.broadcasted_iota(jnp.int32, (rows, pair), 1) < head_dim
    low_side = lax.broadcasted_iota(jnp.int32, (side, pair), 1) < head_dim
    own = (
        lax.broadcasted_iota(jnp.int32, (side, side), 0) // head_dim
        == lax.broadcasted_iota(jnp.int32, (side, side), 1) // BLK
    )
    owner = lax.broadcasted_iota(jnp.int32, (head_dim, side), 1) // BLK
    nothing = jnp.zeros((side, side), BF16)

    def swapped(tile):
        return jnp.concatenate([tile[:, head_dim:], tile[:, :head_dim]], axis=1)

    for tile in range(width // pair):
        span = slice(tile * pair, (tile + 1) * pair)
        for at, dup_ref in enumerate((kd_ref, vd_ref)):
            straight = rows_ref[:, (at + 1) * width + tile * pair :][:, :pair]
            crossed = swapped(straight)
            dup_ref[2 * tile] = jnp.where(low_rows, straight, crossed)
            dup_ref[2 * tile + 1] = jnp.where(low_rows, crossed, straight)
        for at, turn_ref in enumerate((kt_ref, vt_ref)):
            straight = cols_ref[(at + 1) * width : (at + 2) * width, span]
            turn_ref[0, :, span] = straight
            turn_ref[1, :, span] = swapped(straight)

    def diagonal(stack):
        out = stack[:head_dim]
        for at in range(1, group):
            out = jnp.where(owner == at, stack[at * head_dim : (at + 1) * head_dim], out)
        return out

    def pair_step(p, carry):
        at = pl.multiple_of(p * pair, pair)
        totals = []
        for odd in range(2):
            head = 2 * p + odd
            here = pl.multiple_of(at + odd * head_dim, head_dim)
            accs = acc_refs[2 * odd : 2 * odd + 2]
            for acc_ref in accs:
                acc_ref[...] = jnp.zeros_like(acc_ref)
            for part in range(blocks // group):
                span = slice(part * side, (part + 1) * side)
                names = [
                    [lists_ref[head, part * group + a, k] for k in range(listed)]
                    for a in range(group)
                ]
                starts = [[pl.multiple_of(n * BLK, BLK) for n in row] for row in names]
                tiles = [[pl.multiple_of(n // 2 * pair, pair) for n in row] for row in names]

                def gathered(ref):
                    columns = []
                    for b in range(group // 2):
                        pieces = [
                            jnp.where(
                                low,
                                ref[head, pl.ds(starts[2 * b][k], BLK), :],
                                ref[head, pl.ds(starts[2 * b + 1][k], BLK), :],
                            )
                            for k in range(listed)
                        ]
                        columns.append(jnp.concatenate(pieces, axis=0))
                    return jnp.concatenate(columns, axis=1)

                def gathered_t(ref):
                    lines = []
                    for a in range(group):
                        pieces = []
                        for b in range(listed // 2):
                            even, other = names[a][2 * b], names[a][2 * b + 1]
                            pieces.append(
                                jnp.where(
                                    low,
                                    ref[
                                        lax.rem(even, 2),
                                        pl.ds(here, head_dim),
                                        pl.ds(tiles[a][2 * b], pair),
                                    ],
                                    ref[
                                        1 - lax.rem(other, 2),
                                        pl.ds(here, head_dim),
                                        pl.ds(tiles[a][2 * b + 1], pair),
                                    ],
                                )
                            )
                        lines.append(jnp.concatenate(pieces, axis=1))
                    return jnp.concatenate(lines, axis=0)

                def spaced_t(ref):
                    line = ref[pl.ds(here, head_dim), span]
                    return jnp.where(own, jnp.concatenate([line] * group, axis=0), nothing)

                def spaced(tile):
                    crossed = swapped(tile)
                    both = (crossed, tile) if odd else (tile, crossed)
                    line = jnp.where(low_side, *both)
                    return jnp.where(own, jnp.concatenate([line] * (group // 2), axis=1), nothing)

                scores = dot(gathered(kd_ref), spaced_t(cols_ref))
                top = jnp.max(scores, axis=0, keepdims=True)
                expo = jnp.exp2((scores - top) * scale)
                probs = expo * (1.0 / jnp.sum(expo, axis=0, keepdims=True))
                probs_low = probs.astype(BF16)
                attended = diagonal(dot(gathered_t(vt_ref), probs_low))
                left_ref[1, pl.ds(here, head_dim), span] = attended.astype(BF16)
                dprobs = dot(gathered(vd_ref), spaced_t(gat_ref))
                delta = jnp.sum(probs * dprobs, axis=0, keepdims=True)
                dscores = (probs * (dprobs - delta) * factor).astype(BF16)
                dquery = diagonal(dot(gathered_t(kt_ref), dscores))
                dqt_ref[pl.ds(here, head_dim), span] = dquery.astype(BF16)
                dvalues = dot(probs_low, spaced(ga_ref[span, pl.ds(at, pair)]))
                dkeys = dot(dscores, spaced(rows_ref[span, pl.ds(at, pair)]))
                for acc_ref, terms in zip(accs, (dkeys, dvalues)):
                    for k in range(listed):
                        for a in range(group):
                            piece = terms[k * BLK : (k + 1) * BLK, a // 2 * pair : (a // 2 + 1) * pair]
                            piece = jnp.where(low, 0.0, piece) if a % 2 else jnp.where(low, piece, 0.0)
                            acc_ref[pl.ds(starts[a][k], BLK), :] += piece
            totals.append([acc_ref[...] + swapped(acc_ref[...]) for acc_ref in accs])
        for which in range(2):
            both = jnp.where(low_rows, totals[0][which], totals[1][which])
            right_ref[1 + which, :, pl.ds(at, pair)] = both.astype(BF16)
        return carry

    lax.fori_loop(0, HEADS // 2, pair_step, 0, unroll=True)
    right_ref[0] = dqt_ref[...].T
    core, spot = place_ref[0], place_ref[1]
    high = grad_ref.shape[2]
    per = width // high
    copies = []
    for half in (1, 0):
        for slot in list(range(1, spots)) + [0]:
            chunk = lax.rem(spot + slot, spots)
            which = lax.rem(core + half, 2) * (spots // per) + chunk // per
            start = pl.multiple_of(lax.rem(chunk, per) * high, high)
            lhs = left_ref[which // 3, pl.ds(start, high), :]
            grad_ref[half, slot] = dot(lhs, right_ref[which]) * norm
            at = half * spots + slot
            copy = pltpu.make_async_copy(grad_ref.at[half, slot], grad_outs[at], grad_sem.at[at])
            copy.start()
            copies.append(copy)

    attended = left_ref[1].T
    output = x.astype(F32) + dot(attended, wo_ref[...])
    og_ref[0] = output.astype(BF16).reshape(og_ref.shape[1:])
    copies.append(pltpu.make_async_copy(og_ref.at[0], og_out.at[:, 0], og_sem.at[0]))
    copies[-1].start()
    grad_in = g.astype(F32) + dot(right_ref[0], wt_ref[:width, :])
    grad_in = grad_in + dot(right_ref[1], wt_ref[width : 2 * width, :])
    grad_in = grad_in + dot(right_ref[2], wt_ref[2 * width :, :])
    og_ref[1] = grad_in.astype(BF16).reshape(og_ref.shape[1:])
    copies.append(pltpu.make_async_copy(og_ref.at[1], og_out.at[:, 1], og_sem.at[1]))
    copies[-1].start()
    for copy in copies:
        copy.wait()


def column_pass(xg, w, wt, wo, lists, place, norm, spots):
    lat, _, lat_rows, width = xg.shape
    rows = lat * lat_rows
    high = 4 * width // CORES // spots
    whole = pl.BlockSpec(memory_space=pltpu.VMEM)
    return pl.pallas_call(
        functools.partial(column_kernel, norm, spots),
        out_shape=(jax.ShapeDtypeStruct(xg.shape, BF16),)
        + (jax.ShapeDtypeStruct((high, width), F32),) * (2 * spots),
        in_specs=[pl.BlockSpec(memory_space=pltpu.SMEM)]
        + [whole] * 4
        + [pl.BlockSpec(memory_space=pltpu.SMEM)],
        out_specs=(pl.BlockSpec(memory_space=pltpu.HBM),) * (1 + 2 * spots),
        scratch_shapes=[
            pltpu.VMEM((rows, 3 * width), BF16),
            pltpu.VMEM((3 * width, rows), BF16),
            pltpu.VMEM((rows, width), BF16),
            pltpu.VMEM((width, rows), BF16),
            pltpu.VMEM((2, width, rows), BF16),
            pltpu.VMEM((4, rows, width), BF16),
            pltpu.VMEM((width, rows), BF16),
            pltpu.VMEM((HEADS, rows, 2 * width // HEADS), BF16),
            pltpu.VMEM((HEADS, rows, 2 * width // HEADS), BF16),
            pltpu.VMEM((2, width, rows), BF16),
            pltpu.VMEM((2, width, rows), BF16),
            pltpu.VMEM((rows, 2 * width // HEADS), F32),
            pltpu.VMEM((rows, 2 * width // HEADS), F32),
            pltpu.VMEM((rows, 2 * width // HEADS), F32),
            pltpu.VMEM((rows, 2 * width // HEADS), F32),
            pltpu.VMEM((2, lat, lat_rows, width), BF16),
            pltpu.VMEM((2, spots, high, width), F32),
            pltpu.SemaphoreType.DMA((2,)),
            pltpu.SemaphoreType.DMA((2 * spots,)),
        ],
        compiler_params=pltpu.CompilerParams(vmem_limit_bytes=60 * 1024 * 1024),
    )(place, xg, w, wt, wo, lists)


def tiles_kernel(x_in, g_in, out, x_ref, g_ref, tile_ref, in_sem, out_sem):
    arrivals = []
    for at, (source, ref) in enumerate(((x_in, x_ref), (g_in, g_ref))):
        arrivals.append(pltpu.make_async_copy(source, ref, in_sem.at[at]))
        arrivals[-1].start()
    copies = []
    for at, ref in enumerate((x_ref, g_ref)):
        arrivals[at].wait()
        tile_ref[at] = jnp.swapaxes(ref[...], 0, 1)
        copies.append(pltpu.make_async_copy(tile_ref.at[at], out.at[:, at], out_sem.at[at]))
        copies[-1].start()
    for copy in copies:
        copy.wait()


def to_tiles(x, g):
    lat_rows, cols, width = x.shape
    there = pl.BlockSpec(memory_space=pltpu.HBM)
    return pl.pallas_call(
        tiles_kernel,
        out_shape=jax.ShapeDtypeStruct((cols, 2, lat_rows, width), BF16),
        in_specs=[there] * 2,
        out_specs=there,
        scratch_shapes=[
            pltpu.VMEM(x.shape, BF16),
            pltpu.VMEM(x.shape, BF16),
            pltpu.VMEM((2, cols, lat_rows, width), BF16),
            pltpu.SemaphoreType.DMA((2,)),
            pltpu.SemaphoreType.DMA((2,)),
        ],
        compiler_params=pltpu.CompilerParams(vmem_limit_bytes=60 * 1024 * 1024),
    )(x, g)


def settle_kernel(back_ref, *refs):
    ins, out_ref = refs[:-1], refs[-1]
    lat, high, width = out_ref.shape
    for side in range(2):
        first, *others = ins[side * len(ins) // 2 : (side + 1) * len(ins) // 2]
        total = first[...]
        for other_ref in others:
            total = total + other_ref[...]
        out_ref[side * lat // 2 : (side + 1) * lat // 2] = total.reshape(lat // 2, high, width)


def settle(back, uppers, lowers, lat):
    parts = uppers + lowers
    high, width = parts[0].shape
    chunk = pl.BlockSpec((high, width), lambda i: (0, 0))
    shape = (lat, 2 * high // lat, width)
    return pl.pallas_call(
        settle_kernel,
        grid=(1,),
        out_shape=jax.ShapeDtypeStruct(shape, F32),
        in_specs=[pl.BlockSpec(memory_space=pl.ANY)] + [chunk] * len(parts),
        out_specs=pl.BlockSpec(shape, lambda i: (0, 0, 0)),
        compiler_params=pltpu.CompilerParams(vmem_limit_bytes=32 * 1024 * 1024),
    )(back, *parts)


def spread_kernel(spots, place_ref, *refs):
    ins, back_in = refs[: CORES * spots], refs[CORES * spots]
    outs, tile_outs = refs[CORES * spots + 1 : -8], refs[-8:-6]
    wide_ref, back_ref, tile_ref, sem, back_sem, tile_sem = refs[-6:]
    arrive = pltpu.make_async_copy(back_in, back_ref, back_sem)
    arrive.start()
    core, spot = place_ref[0], place_ref[1]
    high = wide_ref.shape[1]
    per = outs[0].shape[0] // high
    copies = []
    for at, in_ref in enumerate(ins):
        far, slot = at // spots, at % spots
        wide_ref[at] = in_ref[...].astype(F32)
        chunk = lax.rem(core + far, CORES) * spots + lax.rem(spot + slot, spots)
        start = pl.multiple_of(lax.rem(chunk, per) * high, high)
        for which, out_ref in enumerate(outs):
            there = out_ref.at[pl.ds(start, high), :]
            copy = pltpu.make_async_copy(wide_ref.at[at], there, sem.at[at])

            @pl.when(chunk // per == which)
            def _():
                copy.start()

        copies.append(copy)
    arrive.wait()
    for at, out_ref in enumerate(tile_outs):
        tile_ref[at] = jnp.swapaxes(back_ref[:, at], 0, 1)
        copy = pltpu.make_async_copy(tile_ref.at[at], out_ref, tile_sem.at[at])
        copy.start()
        copies.append(copy)
    for copy in copies:
        copy.wait()


def spread(parts, back, place, width):
    cols, _, lat_rows, _ = back.shape
    tile = (lat_rows, cols, width)
    whole = pl.BlockSpec(memory_space=pltpu.VMEM)
    there = pl.BlockSpec(memory_space=pltpu.HBM)
    return pl.pallas_call(
        functools.partial(spread_kernel, len(parts) // CORES),
        out_shape=(jax.ShapeDtypeStruct((width, width), F32),) * 4
        + (jax.ShapeDtypeStruct(tile, BF16),) * 2,
        in_specs=[pl.BlockSpec(memory_space=pltpu.SMEM)] + [whole] * len(parts) + [there],
        out_specs=(there,) * 6,
        scratch_shapes=[
            pltpu.VMEM((len(parts),) + parts[0].shape, F32),
            pltpu.VMEM(back.shape, BF16),
            pltpu.VMEM((2,) + tile, BF16),
            pltpu.SemaphoreType.DMA((len(parts),)),
            pltpu.SemaphoreType.DMA,
            pltpu.SemaphoreType.DMA((2,)),
        ],
        compiler_params=pltpu.CompilerParams(vmem_limit_bytes=32 * 1024 * 1024),
    )(place, *parts, back)


def swap_core(item, lon):
    return lax.ppermute(item, "lon", [(i, i ^ 1) for i in range(lon)])


def shift_chip(item, lon, by):
    return lax.ppermute(item, "lon", [(i, (i + by * CORES) % lon) for i in range(lon)])


def per_device(features, grad_out, w_query, w_key, w_value, w_out, block_lists):
    lat_rows, lon_cols, width = features.shape
    lat, lon = lax.axis_size("lat"), lax.axis_size("lon")
    spots = lon // CORES
    norm = 1.0 / math.sqrt(lat_rows * lon_cols * lat * lon)
    index = lax.axis_index("lon")
    place = jnp.stack([lax.rem(index, CORES), index // CORES]).astype(jnp.int32)
    w = jnp.concatenate([w_query, w_key, w_value], axis=1)

    xg = lax.all_to_all(to_tiles(features, grad_out), "lat", 0, 0, tiled=True)
    og, *parts = column_pass(xg, w, w.T, w_out, block_lists, place, norm, spots)
    mine, send = parts[:spots], parts[spots:]
    back = lax.all_to_all(og, "lat", 0, 0, tiled=True)
    taken = [swap_core(send[k], lon) for k in (2, 1, 3, 0)]
    taken = [taken[3], taken[1], taken[0], taken[2]]
    cut = mine[0].shape[0] // 2
    upper = [m[:cut] + t[:cut] for m, t in zip(mine, taken)]
    lower = [m[cut:] + t[cut:] for m, t in zip(mine, taken)]
    from_left, from_right = shift_chip(upper[2], lon, 1), shift_chip(lower[2], lon, spots - 1)
    lower_left, upper_right = shift_chip(lower[1], lon, 1), shift_chip(upper[3], lon, spots - 1)
    upper_left = shift_chip(upper[1] + from_left, lon, 1)
    lower_right = shift_chip(lower[3] + from_right, lon, spots - 1)
    uppers, lowers = [upper[0], upper_right, upper_left], [lower[0], lower_left, lower_right]
    total = settle(back, uppers, lowers, lat)
    total = jnp.sum(lax.all_to_all(total, "lat", 0, 0, tiled=True), axis=0)
    total = jnp.broadcast_to(total.astype(BF16)[None], (lat,) + total.shape)
    own = lax.all_to_all(total, "lat", 0, 0, tiled=True).reshape(-1, width)
    near = [own] + [shift_chip(own, lon, spots - k) for k in range(1, spots)]
    far = [swap_core(item, lon) for item in near]
    *grads, output, grad_in = spread(near + far, back, place, width)
    return (output, grad_in) + tuple(grads)


def solution(mesh):
    tile = P(("member", "lat"), "lon", None)
    in_specs = (tile, tile, P(), P(), P(), P(), P())
    out_specs = (tile, tile) + (P("member", None),) * 4
    return jax.shard_map(
        per_device, mesh=mesh, in_specs=in_specs, out_specs=out_specs, check_vma=False
    )
```

```python
import functools
import math

import jax
import jax.numpy as jnp
from jax import lax
from jax.experimental import pallas as pl
from jax.experimental.pallas import tpu as pltpu
from jax.sharding import PartitionSpec as P

HEADS = 8
BLK = 64
CORES = 2
BF16 = jnp.bfloat16
F32 = jnp.float32
NT = (((1,), (1,)), ((), ()))


def dot(left, right):
    return jnp.dot(left, right, preferred_element_type=F32)


def dot_nt(left, right):
    return lax.dot_general(left, right, NT, preferred_element_type=F32)


def column_kernel(
    norm,
    spots,
    place_ref,
    xg_ref,
    w_ref,
    wt_ref,
    wo_ref,
    lists_ref,
    *refs,
):
    og_out, grad_outs = refs[0], refs[1 : 1 + 2 * spots]
    rows_ref, cols_ref, ga_ref, gat_ref, left_ref, right_ref, dqt_ref = refs[1 + 2 * spots : 8 + 2 * spots]
    kv_ref, vk_ref, kt_ref, vt_ref, *acc_refs = refs[8 + 2 * spots : -4]
    og_ref, grad_ref, og_sem, grad_sem = refs[-4:]
    rows, width = ga_ref.shape
    head_dim = width // HEADS
    pair = 2 * head_dim
    factor = 1.0 / math.sqrt(head_dim)
    scale = factor * math.log2(math.e)
    x = xg_ref[:, 0].reshape(rows, width)
    g = xg_ref[:, 1].reshape(rows, width)
    left_ref[0] = x.T
    right_ref[3] = g

    for part in range(3):
        span = slice(part * width, (part + 1) * width)
        rows_ref[:, span] = dot(x, w_ref[:, span]).astype(BF16)
        cols_ref[span, :] = dot_nt(wt_ref[span, :], x).astype(BF16)
    ga_ref[...] = dot_nt(g, wo_ref[...]).astype(BF16)
    gat_ref[...] = dot_nt(wo_ref[...], g).astype(BF16)

    blocks, listed = lists_ref.shape[1:]
    side = listed * BLK
    group = side // head_dim
    low = lax.broadcasted_iota(jnp.int32, (BLK, pair), 1) < head_dim
    low_rows = lax.broadcasted_iota(jnp.int32, (rows, pair), 1) < head_dim
    low_side = lax.broadcasted_iota(jnp.int32, (side, pair), 1) < head_dim
    own = (
        lax.broadcasted_iota(jnp.int32, (side, side), 0) // head_dim
        == lax.broadcasted_iota(jnp.int32, (side, side), 1) // BLK
    )
    row_part = lax.broadcasted_iota(jnp.int32, (side, side), 0) // head_dim
    lane_part = lax.broadcasted_iota(jnp.int32, (side, side), 1) // BLK
    own_x = row_part + 1 - 2 * lax.rem(row_part, 2) == lane_part
    owner = lax.broadcasted_iota(jnp.int32, (head_dim, side), 1) // BLK
    nothing = jnp.zeros((side, side), BF16)

    def swapped(tile):
        return jnp.concatenate([tile[:, head_dim:], tile[:, :head_dim]], axis=1)

    for tile in range(width // pair):
        span = slice(tile * pair, (tile + 1) * pair)
        keys = rows_ref[:, width + tile * pair :][:, :pair]
        values = rows_ref[:, 2 * width + tile * pair :][:, :pair]
        keys_x, values_x = swapped(keys), swapped(values)
        kv_ref[2 * tile] = jnp.where(low_rows, keys, values_x)
        vk_ref[2 * tile] = jnp.where(low_rows, values, keys_x)
        kv_ref[2 * tile + 1] = jnp.where(low_rows, keys_x, values)
        vk_ref[2 * tile + 1] = jnp.where(low_rows, values_x, keys)
        for at, turn_ref in enumerate((kt_ref, vt_ref)):
            straight = cols_ref[(at + 1) * width : (at + 2) * width, span]
            turn_ref[0, :, span] = straight
            turn_ref[1, :, span] = swapped(straight)

    def diagonal(stack):
        out = stack[:head_dim]
        for at in range(1, group):
            out = jnp.where(owner == at, stack[at * head_dim : (at + 1) * head_dim], out)
        return out

    def names_of(head, part):
        return [
            [lists_ref[head, part * group + a, k] for k in range(listed)] for a in range(group)
        ]

    def gathered(head, starts):
        key_columns, value_columns = [], []
        for b in range(group // 2):
            keys, values = [], []
            for k in range(listed):
                even = kv_ref[head, pl.ds(starts[2 * b][k], BLK), :]
                other = vk_ref[head, pl.ds(starts[2 * b + 1][k], BLK), :]
                keys.append(jnp.where(low, even, other))
                values.append(jnp.where(low, other, even))
            key_columns.append(jnp.concatenate(keys, axis=0))
            value_columns.append(jnp.concatenate(values, axis=0))
        return jnp.concatenate(key_columns, axis=1), jnp.concatenate(value_columns, axis=1)

    def gathered_t(ref, head, names):
        here = slice(head * head_dim, (head + 1) * head_dim)
        lines = []
        for row in names:
            pieces = []
            for even, other in zip(row[::2], row[1::2]):
                tiles = [pl.multiple_of(n // 2 * pair, pair) for n in (even, other)]
                left = ref[lax.rem(even, 2), here, pl.ds(tiles[0], pair)]
                right = ref[1 - lax.rem(other, 2), here, pl.ds(tiles[1], pair)]
                pieces.append(jnp.where(low, left, right))
            lines.append(jnp.concatenate(pieces, axis=1))
        return jnp.concatenate(lines, axis=0)

    def spaced_t(line, mask):
        return jnp.where(mask, jnp.concatenate([line] * group, axis=0), nothing)

    def spaced(tile, odd, mask):
        crossed = swapped(tile)
        line = jnp.where(low_side, *((crossed, tile) if odd else (tile, crossed)))
        return jnp.where(mask, jnp.concatenate([line] * (group // 2), axis=1), nothing)

    def products(head, part):
        here = slice(head * head_dim, (head + 1) * head_dim)
        span = slice(part * side, (part + 1) * side)
        names = names_of(head, part)
        starts = [[pl.multiple_of(n * BLK, BLK) for n in row] for row in names]
        k_rows, v_rows = gathered(head, starts)
        scores = dot(k_rows, spaced_t(cols_ref[here, span], own))
        dprobs = dot(v_rows, spaced_t(gat_ref[here, span], own_x))
        return names, starts, scores, dprobs

    def finish(head, part, accs, names, starts, scores, dprobs):
        here = slice(head * head_dim, (head + 1) * head_dim)
        span = slice(part * side, (part + 1) * side)
        tile = slice(head // 2 * pair, (head // 2 + 1) * pair)
        odd = head % 2
        top = jnp.max(scores, axis=0, keepdims=True)
        expo = jnp.exp2((scores - top) * scale)
        probs = expo * (1.0 / jnp.sum(expo, axis=0, keepdims=True))
        probs_low = probs.astype(BF16)
        delta = jnp.sum(probs * dprobs, axis=0, keepdims=True)
        dscores = (probs * (dprobs - delta) * factor).astype(BF16)
        attended = diagonal(dot(gathered_t(vt_ref, head, names), probs_low))
        left_ref[1, here, span] = attended.astype(BF16)
        dquery = diagonal(dot(gathered_t(kt_ref, head, names), dscores))
        dqt_ref[here, span] = dquery.astype(BF16)
        dvalues = dot(probs_low, spaced(ga_ref[span, tile], odd, own_x))
        dkeys = dot(dscores, spaced(rows_ref[span, tile], odd, own))
        for b in range(group // 2):
            both = slice(b * pair, (b + 1) * pair)
            terms = (
                jnp.where(low_side, dkeys[:, both], dvalues[:, both]),
                jnp.where(low_side, dvalues[:, both], dkeys[:, both]),
            )
            for k in range(listed):
                for acc_ref, term, row in zip(accs, terms, starts[2 * b : 2 * b + 2]):
                    acc_ref[pl.ds(row[k], BLK), :] += term[k * BLK : (k + 1) * BLK]

    units = [(head, part) for head in range(HEADS) for part in range(blocks // group)]
    ready = [products(*units[0])]
    totals = []
    for at, (head, part) in enumerate(units):
        if at + 1 < len(units):
            ready.append(products(*units[at + 1]))
        accs = acc_refs[2 * (head % 2) : 2 * (head % 2) + 2]
        if part == 0:
            for acc_ref in accs:
                acc_ref[...] = jnp.zeros_like(acc_ref)
        finish(head, part, accs, *ready[at])
        if part == blocks // group - 1:
            totals.append(accs[0][...] + swapped(accs[1][...]))
            if head % 2:
                tile = slice(head // 2 * pair, (head // 2 + 1) * pair)
                both = jnp.where(low_rows, totals[-2], swapped(totals[-1]))
                right_ref[1, :, tile] = both.astype(BF16)
                both = jnp.where(low_rows, swapped(totals[-2]), totals[-1])
                right_ref[2, :, tile] = both.astype(BF16)

    right_ref[0] = dqt_ref[...].T
    core, spot = place_ref[0], place_ref[1]
    high = grad_ref.shape[2]
    per = width // high
    copies = []
    for half in (1, 0):
        for slot in list(range(1, spots)) + [0]:
            chunk = lax.rem(spot + slot, spots)
            which = lax.rem(core + half, 2) * (spots // per) + chunk // per
            start = pl.multiple_of(lax.rem(chunk, per) * high, high)
            lhs = left_ref[which // 3, pl.ds(start, high), :]
            grad_ref[half, slot] = dot(lhs, right_ref[which]) * norm
            at = half * spots + slot
            copy = pltpu.make_async_copy(grad_ref.at[half, slot], grad_outs[at], grad_sem.at[at])
            copy.start()
            copies.append(copy)

    attended = left_ref[1].T
    output = x.astype(F32) + dot(attended, wo_ref[...])
    og_ref[0] = output.astype(BF16).reshape(og_ref.shape[1:])
    copies.append(pltpu.make_async_copy(og_ref.at[0], og_out.at[:, 0], og_sem.at[0]))
    copies[-1].start()
    grad_in = g.astype(F32) + dot(right_ref[0], wt_ref[:width, :])
    grad_in = grad_in + dot(right_ref[1], wt_ref[width : 2 * width, :])
    grad_in = grad_in + dot(right_ref[2], wt_ref[2 * width :, :])
    og_ref[1] = grad_in.astype(BF16).reshape(og_ref.shape[1:])
    copies.append(pltpu.make_async_copy(og_ref.at[1], og_out.at[:, 1], og_sem.at[1]))
    copies[-1].start()
    for copy in copies:
        copy.wait()


def column_pass(xg, w, wt, wo, lists, place, norm, spots):
    lat, _, lat_rows, width = xg.shape
    rows = lat * lat_rows
    high = 4 * width // CORES // spots
    whole = pl.BlockSpec(memory_space=pltpu.VMEM)
    return pl.pallas_call(
        functools.partial(column_kernel, norm, spots),
        out_shape=(jax.ShapeDtypeStruct(xg.shape, BF16),)
        + (jax.ShapeDtypeStruct((high, width), F32),) * (2 * spots),
        in_specs=[pl.BlockSpec(memory_space=pltpu.SMEM)]
        + [whole] * 4
        + [pl.BlockSpec(memory_space=pltpu.SMEM)],
        out_specs=(pl.BlockSpec(memory_space=pltpu.HBM),) * (1 + 2 * spots),
        scratch_shapes=[
            pltpu.VMEM((rows, 3 * width), BF16),
            pltpu.VMEM((3 * width, rows), BF16),
            pltpu.VMEM((rows, width), BF16),
            pltpu.VMEM((width, rows), BF16),
            pltpu.VMEM((2, width, rows), BF16),
            pltpu.VMEM((4, rows, width), BF16),
            pltpu.VMEM((width, rows), BF16),
            pltpu.VMEM((HEADS, rows, 2 * width // HEADS), BF16),
            pltpu.VMEM((HEADS, rows, 2 * width // HEADS), BF16),
            pltpu.VMEM((2, width, rows), BF16),
            pltpu.VMEM((2, width, rows), BF16),
            pltpu.VMEM((rows, 2 * width // HEADS), F32),
            pltpu.VMEM((rows, 2 * width // HEADS), F32),
            pltpu.VMEM((rows, 2 * width // HEADS), F32),
            pltpu.VMEM((rows, 2 * width // HEADS), F32),
            pltpu.VMEM((2, lat, lat_rows, width), BF16),
            pltpu.VMEM((2, spots, high, width), F32),
            pltpu.SemaphoreType.DMA((2,)),
            pltpu.SemaphoreType.DMA((2 * spots,)),
        ],
        compiler_params=pltpu.CompilerParams(vmem_limit_bytes=60 * 1024 * 1024),
    )(place, xg, w, wt, wo, lists)


def tiles_kernel(x_in, g_in, out, x_ref, g_ref, tile_ref, in_sem, out_sem):
    arrivals = []
    for at, (source, ref) in enumerate(((x_in, x_ref), (g_in, g_ref))):
        arrivals.append(pltpu.make_async_copy(source, ref, in_sem.at[at]))
        arrivals[-1].start()
    copies = []
    for at, ref in enumerate((x_ref, g_ref)):
        arrivals[at].wait()
        tile_ref[at] = jnp.swapaxes(ref[...], 0, 1)
        copies.append(pltpu.make_async_copy(tile_ref.at[at], out.at[:, at], out_sem.at[at]))
        copies[-1].start()
    for copy in copies:
        copy.wait()


def to_tiles(x, g):
    lat_rows, cols, width = x.shape
    there = pl.BlockSpec(memory_space=pltpu.HBM)
    return pl.pallas_call(
        tiles_kernel,
        out_shape=jax.ShapeDtypeStruct((cols, 2, lat_rows, width), BF16),
        in_specs=[there] * 2,
        out_specs=there,
        scratch_shapes=[
            pltpu.VMEM(x.shape, BF16),
            pltpu.VMEM(x.shape, BF16),
            pltpu.VMEM((2, cols, lat_rows, width), BF16),
            pltpu.SemaphoreType.DMA((2,)),
            pltpu.SemaphoreType.DMA((2,)),
        ],
        compiler_params=pltpu.CompilerParams(vmem_limit_bytes=60 * 1024 * 1024),
    )(x, g)


def settle_kernel(back_ref, *refs):
    ins, out_ref = refs[:-1], refs[-1]
    lat, high, width = out_ref.shape
    for side in range(2):
        first, *others = ins[side * len(ins) // 2 : (side + 1) * len(ins) // 2]
        total = first[...]
        for other_ref in others:
            total = total + other_ref[...]
        out_ref[side * lat // 2 : (side + 1) * lat // 2] = total.reshape(lat // 2, high, width)


def settle(back, uppers, lowers, lat):
    parts = uppers + lowers
    high, width = parts[0].shape
    chunk = pl.BlockSpec((high, width), lambda i: (0, 0))
    shape = (lat, 2 * high // lat, width)
    return pl.pallas_call(
        settle_kernel,
        grid=(1,),
        out_shape=jax.ShapeDtypeStruct(shape, F32),
        in_specs=[pl.BlockSpec(memory_space=pl.ANY)] + [chunk] * len(parts),
        out_specs=pl.BlockSpec(shape, lambda i: (0, 0, 0)),
        compiler_params=pltpu.CompilerParams(vmem_limit_bytes=32 * 1024 * 1024),
    )(back, *parts)


def spread_kernel(spots, place_ref, *refs):
    ins, back_in = refs[: CORES * spots], refs[CORES * spots]
    outs, tile_outs = refs[CORES * spots + 1 : -8], refs[-8:-6]
    wide_ref, back_ref, tile_ref, sem, back_sem, tile_sem = refs[-6:]
    arrive = pltpu.make_async_copy(back_in, back_ref, back_sem)
    arrive.start()
    core, spot = place_ref[0], place_ref[1]
    high = wide_ref.shape[1]
    per = outs[0].shape[0] // high
    copies = []
    for at, in_ref in enumerate(ins):
        far, slot = at // spots, at % spots
        wide_ref[at] = in_ref[...].astype(F32)
        chunk = lax.rem(core + far, CORES) * spots + lax.rem(spot + slot, spots)
        start = pl.multiple_of(lax.rem(chunk, per) * high, high)
        for which, out_ref in enumerate(outs):
            there = out_ref.at[pl.ds(start, high), :]
            copy = pltpu.make_async_copy(wide_ref.at[at], there, sem.at[at])

            @pl.when(chunk // per == which)
            def _():
                copy.start()

        copies.append(copy)
    arrive.wait()
    for at, out_ref in enumerate(tile_outs):
        tile_ref[at] = jnp.swapaxes(back_ref[:, at], 0, 1)
        copy = pltpu.make_async_copy(tile_ref.at[at], out_ref, tile_sem.at[at])
        copy.start()
        copies.append(copy)
    for copy in copies:
        copy.wait()


def spread(parts, back, place, width):
    cols, _, lat_rows, _ = back.shape
    tile = (lat_rows, cols, width)
    whole = pl.BlockSpec(memory_space=pltpu.VMEM)
    there = pl.BlockSpec(memory_space=pltpu.HBM)
    return pl.pallas_call(
        functools.partial(spread_kernel, len(parts) // CORES),
        out_shape=(jax.ShapeDtypeStruct((width, width), F32),) * 4
        + (jax.ShapeDtypeStruct(tile, BF16),) * 2,
        in_specs=[pl.BlockSpec(memory_space=pltpu.SMEM)] + [whole] * len(parts) + [there],
        out_specs=(there,) * 6,
        scratch_shapes=[
            pltpu.VMEM((len(parts),) + parts[0].shape, F32),
            pltpu.VMEM(back.shape, BF16),
            pltpu.VMEM((2,) + tile, BF16),
            pltpu.SemaphoreType.DMA((len(parts),)),
            pltpu.SemaphoreType.DMA,
            pltpu.SemaphoreType.DMA((2,)),
        ],
        compiler_params=pltpu.CompilerParams(vmem_limit_bytes=32 * 1024 * 1024),
    )(place, *parts, back)


def swap_core(item, lon):
    return lax.ppermute(item, "lon", [(i, i ^ 1) for i in range(lon)])


def shift_chip(item, lon, by):
    return lax.ppermute(item, "lon", [(i, (i + by * CORES) % lon) for i in range(lon)])


def per_device(features, grad_out, w_query, w_key, w_value, w_out, block_lists):
    lat_rows, lon_cols, width = features.shape
    lat, lon = lax.axis_size("lat"), lax.axis_size("lon")
    spots = lon // CORES
    norm = 1.0 / math.sqrt(lat_rows * lon_cols * lat * lon)
    index = lax.axis_index("lon")
    place = jnp.stack([lax.rem(index, CORES), index // CORES]).astype(jnp.int32)
    w = jnp.concatenate([w_query, w_key, w_value], axis=1)

    xg = lax.all_to_all(to_tiles(features, grad_out), "lat", 0, 0, tiled=True)
    og, *parts = column_pass(xg, w, w.T, w_out, block_lists, place, norm, spots)
    mine, send = parts[:spots], parts[spots:]
    back = lax.all_to_all(og, "lat", 0, 0, tiled=True)
    taken = [swap_core(send[k], lon) for k in (2, 1, 3, 0)]
    taken = [taken[3], taken[1], taken[0], taken[2]]
    cut = mine[0].shape[0] // 2
    upper = [m[:cut] + t[:cut] for m, t in zip(mine, taken)]
    lower = [m[cut:] + t[cut:] for m, t in zip(mine, taken)]
    from_left, from_right = shift_chip(upper[2], lon, 1), shift_chip(lower[2], lon, spots - 1)
    lower_left, upper_right = shift_chip(lower[1], lon, 1), shift_chip(upper[3], lon, spots - 1)
    upper_left = shift_chip(upper[1] + from_left, lon, 1)
    lower_right = shift_chip(lower[3] + from_right, lon, spots - 1)
    uppers, lowers = [upper[0], upper_right, upper_left], [lower[0], lower_left, lower_right]
    total = settle(back, uppers, lowers, lat)
    total = jnp.sum(lax.all_to_all(total, "lat", 0, 0, tiled=True), axis=0)
    total = jnp.broadcast_to(total.astype(BF16)[None], (lat,) + total.shape)
    own = lax.all_to_all(total, "lat", 0, 0, tiled=True).reshape(-1, width)
    near = [own] + [shift_chip(own, lon, spots - k) for k in range(1, spots)]
    far = [swap_core(item, lon) for item in near]
    *grads, output, grad_in = spread(near + far, back, place, width)
    return (output, grad_in) + tuple(grads)


def solution(mesh):
    tile = P(("member", "lat"), "lon", None)
    in_specs = (tile, tile, P(), P(), P(), P(), P())
    out_specs = (tile, tile) + (P("member", None),) * 4
    return jax.shard_map(
        per_device, mesh=mesh, in_specs=in_specs, out_specs=out_specs, check_vma=False
    )
```

```python
import functools
import math

import jax
import jax.numpy as jnp
from jax import lax
from jax.experimental import pallas as pl
from jax.experimental.pallas import tpu as pltpu
from jax.sharding import PartitionSpec as P

HEADS = 8
BLK = 64
CORES = 2
BF16 = jnp.bfloat16
F32 = jnp.float32
NT = (((1,), (1,)), ((), ()))


def dot(left, right):
    return jnp.dot(left, right, preferred_element_type=F32)


def dot_nt(left, right):
    return lax.dot_general(left, right, NT, preferred_element_type=F32)


def column_kernel(
    norm,
    spots,
    place_ref,
    xg_ref,
    w_ref,
    wt_ref,
    wo_ref,
    lists_ref,
    *refs,
):
    og_out, grad_outs = refs[0], refs[1 : 1 + 2 * spots]
    rows_ref, cols_ref, ga_ref, gat_ref, left_ref, right_ref, dqt_ref = refs[1 + 2 * spots : 8 + 2 * spots]
    kv_ref, vk_ref, kt_ref, vt_ref, *acc_refs = refs[8 + 2 * spots : -4]
    og_ref, grad_ref, og_sem, grad_sem = refs[-4:]
    rows, width = ga_ref.shape
    head_dim = width // HEADS
    pair = 2 * head_dim
    factor = 1.0 / math.sqrt(head_dim)
    scale = factor * math.log2(math.e)
    x = xg_ref[:, 0].reshape(rows, width)
    g = xg_ref[:, 1].reshape(rows, width)
    left_ref[0] = x.T
    right_ref[3] = g

    for part in range(3):
        span = slice(part * width, (part + 1) * width)
        rows_ref[:, span] = dot(x, w_ref[:, span]).astype(BF16)
        cols_ref[span, :] = dot_nt(wt_ref[span, :], x).astype(BF16)
    ga_ref[...] = dot_nt(g, wo_ref[...]).astype(BF16)
    gat_ref[...] = dot_nt(wo_ref[...], g).astype(BF16)

    blocks, listed = lists_ref.shape[1:]
    side = listed * BLK
    group = side // head_dim
    low = lax.broadcasted_iota(jnp.int32, (BLK, pair), 1) < head_dim
    low_rows = lax.broadcasted_iota(jnp.int32, (rows, pair), 1) < head_dim
    low_side = lax.broadcasted_iota(jnp.int32, (side, pair), 1) < head_dim
    own = (
        lax.broadcasted_iota(jnp.int32, (side, side), 0) // head_dim
        == lax.broadcasted_iota(jnp.int32, (side, side), 1) // BLK
    )
    row_part = lax.broadcasted_iota(jnp.int32, (side, side), 0) // head_dim
    lane_part = lax.broadcasted_iota(jnp.int32, (side, side), 1) // BLK
    own_x = row_part + 1 - 2 * lax.rem(row_part, 2) == lane_part
    owner = lax.broadcasted_iota(jnp.int32, (head_dim, side), 1) // BLK
    nothing = jnp.zeros((side, side), BF16)

    def swapped(tile):
        return jnp.concatenate([tile[:, head_dim:], tile[:, :head_dim]], axis=1)

    for tile in range(width // pair):
        span = slice(tile * pair, (tile + 1) * pair)
        keys = rows_ref[:, width + tile * pair :][:, :pair]
        values = rows_ref[:, 2 * width + tile * pair :][:, :pair]
        keys_x, values_x = swapped(keys), swapped(values)
        kv_ref[2 * tile] = jnp.where(low_rows, keys, values_x)
        vk_ref[2 * tile] = jnp.where(low_rows, values, keys_x)
        kv_ref[2 * tile + 1] = jnp.where(low_rows, keys_x, values)
        vk_ref[2 * tile + 1] = jnp.where(low_rows, values_x, keys)
        for at, turn_ref in enumerate((kt_ref, vt_ref)):
            straight = cols_ref[(at + 1) * width : (at + 2) * width, span]
            turn_ref[0, :, span] = straight
            turn_ref[1, :, span] = swapped(straight)

    def diagonal(stack):
        out = stack[:head_dim]
        for at in range(1, group):
            out = jnp.where(owner == at, stack[at * head_dim : (at + 1) * head_dim], out)
        return out

    def names_of(head, part):
        return [
            [lists_ref[head, part * group + a, k] for k in range(listed)] for a in range(group)
        ]

    def gathered(head, starts):
        key_columns, value_columns = [], []
        for b in range(group // 2):
            keys, values = [], []
            for k in range(listed):
                even = kv_ref[head, pl.ds(starts[2 * b][k], BLK), :]
                other = vk_ref[head, pl.ds(starts[2 * b + 1][k], BLK), :]
                keys.append(jnp.where(low, even, other))
                values.append(jnp.where(low, other, even))
            key_columns.append(jnp.concatenate(keys, axis=0))
            value_columns.append(jnp.concatenate(values, axis=0))
        return jnp.concatenate(key_columns, axis=1), jnp.concatenate(value_columns, axis=1)

    def gathered_t(ref, head, names):
        here = slice(head * head_dim, (head + 1) * head_dim)
        lines = []
        for row in names:
            pieces = []
            for even, other in zip(row[::2], row[1::2]):
                tiles = [pl.multiple_of(n // 2 * pair, pair) for n in (even, other)]
                left = ref[lax.rem(even, 2), here, pl.ds(tiles[0], pair)]
                right = ref[1 - lax.rem(other, 2), here, pl.ds(tiles[1], pair)]
                pieces.append(jnp.where(low, left, right))
            lines.append(jnp.concatenate(pieces, axis=1))
        return jnp.concatenate(lines, axis=0)

    def spaced_t(line, mask):
        return jnp.where(mask, jnp.concatenate([line] * group, axis=0), nothing)

    def spaced(tile, odd, mask):
        crossed = swapped(tile)
        line = jnp.where(low_side, *((crossed, tile) if odd else (tile, crossed)))
        return jnp.where(mask, jnp.concatenate([line] * (group // 2), axis=1), nothing)

    def products(head, part):
        here = slice(head * head_dim, (head + 1) * head_dim)
        span = slice(part * side, (part + 1) * side)
        names = names_of(head, part)
        starts = [[pl.multiple_of(n * BLK, BLK) for n in row] for row in names]
        k_rows, v_rows = gathered(head, starts)
        scores = dot(k_rows, spaced_t(cols_ref[here, span], own))
        dprobs = dot(v_rows, spaced_t(gat_ref[here, span], own_x))
        return names, starts, scores, dprobs

    def finish(head, part, accs, names, starts, scores, dprobs):
        here = slice(head * head_dim, (head + 1) * head_dim)
        span = slice(part * side, (part + 1) * side)
        tile = slice(head // 2 * pair, (head // 2 + 1) * pair)
        odd = head % 2
        top = jnp.max(scores, axis=0, keepdims=True)
        expo = jnp.exp2((scores - top) * scale)
        probs = expo * (1.0 / jnp.sum(expo, axis=0, keepdims=True))
        probs_low = probs.astype(BF16)
        delta = jnp.sum(probs * dprobs, axis=0, keepdims=True)
        dscores = (probs * (dprobs - delta) * factor).astype(BF16)
        attended = diagonal(dot(gathered_t(vt_ref, head, names), probs_low))
        left_ref[1, here, span] = attended.astype(BF16)
        dquery = diagonal(dot(gathered_t(kt_ref, head, names), dscores))
        dqt_ref[here, span] = dquery.astype(BF16)
        dvalues = dot(probs_low, spaced(ga_ref[span, tile], odd, own_x))
        dkeys = dot(dscores, spaced(rows_ref[span, tile], odd, own))
        for b in range(group // 2):
            both = slice(b * pair, (b + 1) * pair)
            terms = (
                jnp.where(low_side, dkeys[:, both], dvalues[:, both]),
                jnp.where(low_side, dvalues[:, both], dkeys[:, both]),
            )
            for k in range(listed):
                for acc_ref, term, row in zip(accs, terms, starts[2 * b : 2 * b + 2]):
                    acc_ref[pl.ds(row[k], BLK), :] += term[k * BLK : (k + 1) * BLK]

    units = [(head, part) for head in range(HEADS) for part in range(blocks // group)]
    ready = [products(*units[0])]
    totals = []
    for at, (head, part) in enumerate(units):
        if at + 1 < len(units):
            ready.append(products(*units[at + 1]))
        accs = acc_refs[2 * (head % 2) : 2 * (head % 2) + 2]
        if part == 0:
            for acc_ref in accs:
                acc_ref[...] = jnp.zeros_like(acc_ref)
        finish(head, part, accs, *ready[at])
        if part == blocks // group - 1:
            totals.append(accs[0][...] + swapped(accs[1][...]))
            if head % 2:
                tile = slice(head // 2 * pair, (head // 2 + 1) * pair)
                both = jnp.where(low_rows, totals[-2], swapped(totals[-1]))
                right_ref[1, :, tile] = both.astype(BF16)
                both = jnp.where(low_rows, swapped(totals[-2]), totals[-1])
                right_ref[2, :, tile] = both.astype(BF16)

    right_ref[0] = dqt_ref[...].T
    core, spot = place_ref[0], place_ref[1]
    high = grad_ref.shape[2]
    per = width // high
    copies = []
    for half in (1, 0):
        for slot in list(range(1, spots)) + [0]:
            chunk = lax.rem(spot + slot, spots)
            which = lax.rem(core + half, 2) * (spots // per) + chunk // per
            start = pl.multiple_of(lax.rem(chunk, per) * high, high)
            lhs = left_ref[which // 3, pl.ds(start, high), :]
            grad_ref[half, slot] = dot(lhs, right_ref[which]) * norm
            at = half * spots + slot
            copy = pltpu.make_async_copy(grad_ref.at[half, slot], grad_outs[at], grad_sem.at[at])
            copy.start()
            copies.append(copy)

    attended = left_ref[1].T
    output = x.astype(F32) + dot(attended, wo_ref[...])
    og_ref[0] = output.astype(BF16).reshape(og_ref.shape[1:])
    copies.append(pltpu.make_async_copy(og_ref.at[0], og_out.at[:, 0], og_sem.at[0]))
    copies[-1].start()
    grad_in = g.astype(F32) + dot(right_ref[0], wt_ref[:width, :])
    grad_in = grad_in + dot(right_ref[1], wt_ref[width : 2 * width, :])
    grad_in = grad_in + dot(right_ref[2], wt_ref[2 * width :, :])
    og_ref[1] = grad_in.astype(BF16).reshape(og_ref.shape[1:])
    copies.append(pltpu.make_async_copy(og_ref.at[1], og_out.at[:, 1], og_sem.at[1]))
    copies[-1].start()
    for copy in copies:
        copy.wait()


def column_pass(xg, w, wt, wo, lists, place, norm, spots):
    lat, _, lat_rows, width = xg.shape
    rows = lat * lat_rows
    high = 4 * width // CORES // spots
    whole = pl.BlockSpec(memory_space=pltpu.VMEM)
    return pl.pallas_call(
        functools.partial(column_kernel, norm, spots),
        out_shape=(jax.ShapeDtypeStruct(xg.shape, BF16),)
        + (jax.ShapeDtypeStruct((high, width), F32),) * (2 * spots),
        in_specs=[pl.BlockSpec(memory_space=pltpu.SMEM)]
        + [whole] * 4
        + [pl.BlockSpec(memory_space=pltpu.SMEM)],
        out_specs=(pl.BlockSpec(memory_space=pltpu.HBM),) * (1 + 2 * spots),
        scratch_shapes=[
            pltpu.VMEM((rows, 3 * width), BF16),
            pltpu.VMEM((3 * width, rows), BF16),
            pltpu.VMEM((rows, width), BF16),
            pltpu.VMEM((width, rows), BF16),
            pltpu.VMEM((2, width, rows), BF16),
            pltpu.VMEM((4, rows, width), BF16),
            pltpu.VMEM((width, rows), BF16),
            pltpu.VMEM((HEADS, rows, 2 * width // HEADS), BF16),
            pltpu.VMEM((HEADS, rows, 2 * width // HEADS), BF16),
            pltpu.VMEM((2, width, rows), BF16),
            pltpu.VMEM((2, width, rows), BF16),
            pltpu.VMEM((rows, 2 * width // HEADS), F32),
            pltpu.VMEM((rows, 2 * width // HEADS), F32),
            pltpu.VMEM((rows, 2 * width // HEADS), F32),
            pltpu.VMEM((rows, 2 * width // HEADS), F32),
            pltpu.VMEM((2, lat, lat_rows, width), BF16),
            pltpu.VMEM((2, spots, high, width), F32),
            pltpu.SemaphoreType.DMA((2,)),
            pltpu.SemaphoreType.DMA((2 * spots,)),
        ],
        compiler_params=pltpu.CompilerParams(vmem_limit_bytes=60 * 1024 * 1024),
    )(place, xg, w, wt, wo, lists)


def tiles_kernel(x_in, g_in, out, x_ref, g_ref, tile_ref, in_sem, out_sem):
    arrivals = []
    for at, (source, ref) in enumerate(((x_in, x_ref), (g_in, g_ref))):
        arrivals.append(pltpu.make_async_copy(source, ref, in_sem.at[at]))
        arrivals[-1].start()
    copies = []
    for at, ref in enumerate((x_ref, g_ref)):
        arrivals[at].wait()
        tile_ref[at] = jnp.swapaxes(ref[...], 0, 1)
        copies.append(pltpu.make_async_copy(tile_ref.at[at], out.at[:, at], out_sem.at[at]))
        copies[-1].start()
    for copy in copies:
        copy.wait()


def to_tiles(x, g):
    lat_rows, cols, width = x.shape
    there = pl.BlockSpec(memory_space=pltpu.HBM)
    return pl.pallas_call(
        tiles_kernel,
        out_shape=jax.ShapeDtypeStruct((cols, 2, lat_rows, width), BF16),
        in_specs=[there] * 2,
        out_specs=there,
        scratch_shapes=[
            pltpu.VMEM(x.shape, BF16),
            pltpu.VMEM(x.shape, BF16),
            pltpu.VMEM((2, cols, lat_rows, width), BF16),
            pltpu.SemaphoreType.DMA((2,)),
            pltpu.SemaphoreType.DMA((2,)),
        ],
        compiler_params=pltpu.CompilerParams(vmem_limit_bytes=60 * 1024 * 1024),
    )(x, g)


def settle_kernel(back_ref, *refs):
    ins, out_ref = refs[:-1], refs[-1]
    lat, high, width = out_ref.shape
    for side in range(2):
        first, *others = ins[side * len(ins) // 2 : (side + 1) * len(ins) // 2]
        total = first[...]
        for other_ref in others:
            total = total + other_ref[...]
        out_ref[side * lat // 2 : (side + 1) * lat // 2] = total.reshape(lat // 2, high, width)


def settle(back, uppers, lowers, lat):
    parts = uppers + lowers
    high, width = parts[0].shape
    chunk = pl.BlockSpec((high, width), lambda i: (0, 0))
    shape = (lat, 2 * high // lat, width)
    return pl.pallas_call(
        settle_kernel,
        grid=(1,),
        out_shape=jax.ShapeDtypeStruct(shape, F32),
        in_specs=[pl.BlockSpec(memory_space=pl.ANY)] + [chunk] * len(parts),
        out_specs=pl.BlockSpec(shape, lambda i: (0, 0, 0)),
        compiler_params=pltpu.CompilerParams(vmem_limit_bytes=32 * 1024 * 1024),
    )(back, *parts)


def spread_kernel(spots, place_ref, *refs):
    ins, outs = refs[: CORES * spots], refs[CORES * spots : -2]
    wide_ref, sem = refs[-2:]
    core, spot = place_ref[0], place_ref[1]
    high = wide_ref.shape[1]
    per = outs[0].shape[0] // high
    copies = []
    for at, in_ref in enumerate(ins):
        far, slot = at // spots, at % spots
        wide_ref[at] = in_ref[...].astype(F32)
        chunk = lax.rem(core + far, CORES) * spots + lax.rem(spot + slot, spots)
        start = pl.multiple_of(lax.rem(chunk, per) * high, high)
        for which, out_ref in enumerate(outs):
            there = out_ref.at[pl.ds(start, high), :]
            copy = pltpu.make_async_copy(wide_ref.at[at], there, sem.at[at])

            @pl.when(chunk // per == which)
            def _():
                copy.start()

        copies.append(copy)
    for copy in copies:
        copy.wait()


def spread(parts, place, width):
    whole = pl.BlockSpec(memory_space=pltpu.VMEM)
    there = pl.BlockSpec(memory_space=pltpu.HBM)
    return pl.pallas_call(
        functools.partial(spread_kernel, len(parts) // CORES),
        out_shape=(jax.ShapeDtypeStruct((width, width), F32),) * 4,
        in_specs=[pl.BlockSpec(memory_space=pltpu.SMEM)] + [whole] * len(parts),
        out_specs=(there,) * 4,
        scratch_shapes=[
            pltpu.VMEM((len(parts),) + parts[0].shape, F32),
            pltpu.SemaphoreType.DMA((len(parts),)),
        ],
        compiler_params=pltpu.CompilerParams(vmem_limit_bytes=32 * 1024 * 1024),
    )(place, *parts)


def rows_kernel(back_ref, x_ref, g_ref):
    x_ref[...] = jnp.swapaxes(back_ref[:, 0], 0, 1)
    g_ref[...] = jnp.swapaxes(back_ref[:, 1], 0, 1)


def to_rows(back):
    cols, _, lat_rows, width = back.shape
    whole = pl.BlockSpec(memory_space=pltpu.VMEM)
    return pl.pallas_call(
        rows_kernel,
        out_shape=(jax.ShapeDtypeStruct((lat_rows, cols, width), BF16),) * 2,
        in_specs=[whole],
        out_specs=(whole,) * 2,
        compiler_params=pltpu.CompilerParams(vmem_limit_bytes=32 * 1024 * 1024),
        cost_estimate=pl.CostEstimate(flops=1 << 33, bytes_accessed=32 << 20, transcendentals=0),
    )(back)


def swap_core(item, lon):
    return lax.ppermute(item, "lon", [(i, i ^ 1) for i in range(lon)])


def shift_chip(item, lon, by):
    return lax.ppermute(item, "lon", [(i, (i + by * CORES) % lon) for i in range(lon)])


def per_device(features, grad_out, w_query, w_key, w_value, w_out, block_lists):
    lat_rows, lon_cols, width = features.shape
    lat, lon = lax.axis_size("lat"), lax.axis_size("lon")
    spots = lon // CORES
    norm = 1.0 / math.sqrt(lat_rows * lon_cols * lat * lon)
    index = lax.axis_index("lon")
    place = jnp.stack([lax.rem(index, CORES), index // CORES]).astype(jnp.int32)
    w = jnp.concatenate([w_query, w_key, w_value], axis=1)

    xg = lax.all_to_all(to_tiles(features, grad_out), "lat", 0, 0, tiled=True)
    og, *parts = column_pass(xg, w, w.T, w_out, block_lists, place, norm, spots)
    mine, send = parts[:spots], parts[spots:]
    back = lax.all_to_all(og, "lat", 0, 0, tiled=True)
    taken = [swap_core(send[k], lon) for k in (2, 1, 3, 0)]
    taken = [taken[3], taken[1], taken[0], taken[2]]
    cut = mine[0].shape[0] // 2
    upper = [m[:cut] + t[:cut] for m, t in zip(mine, taken)]
    lower = [m[cut:] + t[cut:] for m, t in zip(mine, taken)]
    from_left, from_right = shift_chip(upper[2], lon, 1), shift_chip(lower[2], lon, spots - 1)
    lower_left, upper_right = shift_chip(lower[1], lon, 1), shift_chip(upper[3], lon, spots - 1)
    upper_left = shift_chip(upper[1] + from_left, lon, 1)
    lower_right = shift_chip(lower[3] + from_right, lon, spots - 1)
    uppers, lowers = [upper[0], upper_right, upper_left], [lower[0], lower_left, lower_right]
    total = settle(back, uppers, lowers, lat)
    total = jnp.sum(lax.all_to_all(total, "lat", 0, 0, tiled=True), axis=0)
    total = jnp.broadcast_to(total.astype(BF16)[None], (lat,) + total.shape)
    own = lax.all_to_all(total, "lat", 0, 0, tiled=True).reshape(-1, width)
    near = [own] + [shift_chip(own, lon, spots - k) for k in range(1, spots)]
    far = [swap_core(item, lon) for item in near]
    output, grad_in = to_rows(back)
    grads = spread(near + far, place, width)
    return (output, grad_in) + tuple(grads)


def solution(mesh):
    tile = P(("member", "lat"), "lon", None)
    in_specs = (tile, tile, P(), P(), P(), P(), P())
    out_specs = (tile, tile) + (P("member", None),) * 4
    return jax.shard_map(
        per_device, mesh=mesh, in_specs=in_specs, out_specs=out_specs, check_vma=False
    )
```
